32 devices in a mesh: row: 4 (over x, core), col: 4 (over z), depth: 2 (over y).
Axes of the slice: x: 2, y: 2, z: 4, core: 2. Of those that a mesh axis runs over, the one named last changes fastest.
Arguments:
- left_blocks: float32 [512, 64, 64], P(('row', 'col', 'depth')), may hold values from -6 to 6
- right_blocks: float32 [512, 64, 64], P(('row', 'col', 'depth')), may hold values from -0.25 to 0.25
- triples: int32 [3, 16384], P(None, ('row', 'col', 'depth')), may hold values from 0 to 128, as said below
Outputs:
- product_blocks: float32 [2048, 64, 64], P(('row', 'col', 'depth'))
The draws below stay inside these ranges and needn't reach their ends.
Inputs may be any that keep to these rules, and one draw needn't show every extreme that they name: With G = 4 contraction groups per panel and layer, left slot number i * G + g is the block of block row i and group g, and right slot j * G + g the block of group g and block column j. Each device keeps 128 distinct (block row, block column) pairs, and out slot o names the o-th of them. A used triple takes the left block (i, g) and the right block (g, j) of one group g and sends their product to the kept slot of (i, j); a device's used triples are distinct and come first among its 512. An unused triple is (0, 0, 128). Every device has at least 128 used triples, and some device has all 512 used.
All inputs are finite; a program needn't handle non-finite values.
Results may differ from the reference program's by a relative error of at most 0.0003.
Values sent between devices are 32-bit elements; how exact they have to be, the bound alone decides.
A program may use at most 128 MiB of HBM per device.

```python
import jax
import jax.numpy as jnp
from jax import lax

BS = 64
SA = 16
PC = 128
MAXT = 512
A_BLOCKS = 512
N_ROW = 4
N_COL = 4
N_DEPTH = 2
DEVICES = 32


def draw_triples(key, part):
    key = jax.random.fold_in(key, 7)
    groups = max(1, SA // 4)
    block_rows = N_COL * SA // groups
    block_cols = N_ROW * SA // groups
    pair_total = block_rows * block_cols
    cand_total = PC * groups
    key_pairs, key_cands, key_live = jax.random.split(key, 3)
    pair_keys = jax.random.split(key_pairs, DEVICES)
    cand_keys = jax.random.split(key_cands, DEVICES)
    pairs = jax.vmap(lambda one: jax.random.permutation(one, pair_total))(pair_keys)
    pairs = (pairs - pairs[:, :1] + pair_total - 1) % pair_total
    pairs = pairs[:, :PC]
    cands = jax.vmap(lambda one: jax.random.permutation(one, cand_total))(cand_keys)
    cands = (cands - cands[:, :1] + groups - 1) % cand_total
    cands = cands[:, :MAXT]
    out_slot = cands // groups
    group_at = cands % groups
    chosen = jnp.take_along_axis(pairs, out_slot, axis=1)
    row_at = chosen // block_cols
    col_at = chosen % block_cols
    left_slot = row_at * groups + group_at
    right_slot = col_at * groups + group_at
    live_count = jax.random.randint(key_live, (DEVICES,), MAXT // 4, MAXT + 1)
    live_count = live_count.at[0].set(MAXT)
    live_count = live_count.at[DEVICES - 1].set(MAXT // 4)
    position = jnp.arange(MAXT)
    keep = position[None, :] < live_count[:, None]
    left_slot = jnp.where(keep, left_slot, 0)
    right_slot = jnp.where(keep, right_slot, 0)
    out_slot = jnp.where(keep, out_slot, PC)
    stacked = jnp.stack([left_slot.reshape(-1), right_slot.reshape(-1), out_slot.reshape(-1)])
    return stacked.astype(jnp.int32)


def block_scale(key, dims, shards, smallest, top_value):
    def one(dim, shards_of):
        steps = jax.random.uniform(jax.random.fold_in(jax.random.fold_in(key, 6), dim), (shards_of,), jnp.float32, smallest / len(shards), top_value / len(shards))
        return jnp.repeat(jnp.exp(steps), dims[dim] // shards_of).reshape((-1,) + (1,) * (len(dims) - dim - 1))

    factor_of = one(*shards[0])
    for cut in shards[1:]:
        factor_of = factor_of * one(*cut)
    return factor_of


def noise(own_key, shape, deviation, most, cuts=(), kind=jnp.bfloat16):
    entries = deviation * jax.random.normal(own_key, shape, jnp.float32)
    if cuts:
        entries = entries * block_scale(own_key, shape, cuts, -0.22, 0.18)
    return jnp.clip(entries, -most, most).astype(kind)


def setup_inputs(seed: int = 0) -> dict:
    key_list = jax.random.split(jax.random.key(seed), 4)
    return {
        "left_blocks": noise(key_list[0], (A_BLOCKS, BS, BS), 1.0, 6.0, ((0, 32),), jnp.float32),
        "right_blocks": noise(key_list[1], (A_BLOCKS, BS, BS), (BS * MAXT * N_DEPTH // PC) ** -0.5, 0.25, ((0, 32),), jnp.float32),
        "triples": draw_triples(jax.random.fold_in(key_list[3], 71), 0),
    }


def reference(left_blocks, right_blocks, triples):
    left_all = left_blocks.reshape(N_ROW, N_COL, N_DEPTH, SA, BS, BS)
    right_all = right_blocks.reshape(N_ROW, N_COL, N_DEPTH, SA, BS, BS)
    slot_all = triples.reshape(3, N_ROW, N_COL, N_DEPTH, MAXT)

    def one_panel(flat):
        row_at = flat // N_COL
        col_at = flat % N_COL

        def layer(total, depth_at):
            left_panel = left_all[row_at, :, depth_at].reshape(N_COL * SA, BS, BS)
            right_panel = right_all[:, col_at, depth_at].reshape(N_ROW * SA, BS, BS)
            picks = slot_all[:, row_at, col_at, depth_at]
            products = jnp.einsum("tij,tjk->tik", left_panel[picks[0]], right_panel[picks[1]], precision=lax.Precision.HIGHEST, preferred_element_type=jnp.float32)
            return total.at[picks[2]].add(products), None

        start_total = jnp.zeros((PC + 1, BS, BS), jnp.float32)
        total, unused = lax.scan(layer, start_total, jnp.arange(N_DEPTH, dtype=jnp.int32))
        return total[:PC]

    panels = lax.map(one_panel, jnp.arange(N_ROW * N_COL, dtype=jnp.int32))
    return panels.reshape(N_ROW * N_COL * PC, BS, BS)
```

```python
import functools

import jax
import jax.numpy as jnp
from jax import lax
from jax.experimental import pallas as pl
from jax.experimental.pallas import tpu as pltpu
from jax.sharding import PartitionSpec as P

PC = 128
LANES = 128
CHUNK_ROWS = 16
UNROLL_PAIRS = 8
MESH = pl.DeviceIdType.MESH


def split_bf16(value):
    high = value.astype(jnp.bfloat16)
    low = (value - high.astype(jnp.float32)).astype(jnp.bfloat16)
    return high, low


def kernel(
    sizes,
    left_ref,
    right_ref,
    triples_ref,
    out_ref,
    left_all,
    right_all,
    right_split,
    left_split,
    mask_ref,
    mask_rows,
    code_rows,
    codes,
    part_send,
    part_recv,
    part_own,
    left_send_sem,
    left_recv_sem,
    right_send_sem,
    right_recv_sem,
    core_send_sem,
    core_recv_sem,
    part_send_sem,
    part_recv_sem,
    code_sem,
):
    n_row, n_col, n_depth, order, groups, local_rows, share, chunks = sizes
    row = lax.axis_index("row")
    col = lax.axis_index("col")
    depth = lax.axis_index("depth")
    outers = n_row // 2
    core = row % 2
    outer = row // 2
    other_core = outer * 2 + (1 - core)
    width = groups * order
    pairs = share // 2

    def turn(index, step, count):
        return lax.rem(index + step, count)

    barrier = pltpu.get_barrier_semaphore()
    greeted = 0
    for step in range(1, n_col):
        pl.semaphore_signal(barrier, inc=1, device_id={"col": turn(col, step, n_col)}, device_id_type=MESH)
        greeted += 1
    for step in range(1, outers):
        pl.semaphore_signal(
            barrier, inc=1, device_id={"row": turn(outer, step, outers) * 2 + core}, device_id_type=MESH
        )
        greeted += 1
    pl.semaphore_signal(barrier, inc=1, device_id={"row": other_core}, device_id_type=MESH)
    greeted += 1
    for step in range(1, n_depth):
        pl.semaphore_signal(barrier, inc=1, device_id={"depth": turn(depth, step, n_depth)}, device_id_type=MESH)
        greeted += 1

    for i in range(local_rows):
        for g in range(0, groups, 2):
            pair = jnp.concatenate([left_ref[i * groups + g], left_ref[i * groups + g + 1]], axis=-1)
            for q in range(chunks):
                left_all[q, col, i, :, g * order : (g + 2) * order] = pair[q * CHUNK_ROWS : (q + 1) * CHUNK_ROWS]
    for j in range(0, local_rows, 2):
        for g in range(groups):
            pair = jnp.concatenate([right_ref[j * groups + g], right_ref[(j + 1) * groups + g]], axis=-1)
            right_all[row, j // 2, g * order : (g + 1) * order, :] = pair

    pl.semaphore_wait(barrier, greeted)

    def left_copy(q, step):
        return pltpu.make_async_remote_copy(
            src_ref=left_all.at[q, col],
            dst_ref=left_all.at[q, col],
            send_sem=left_send_sem.at[q, step - 1],
            recv_sem=left_recv_sem.at[q, step - 1],
            device_id={"col": turn(col, step, n_col)},
            device_id_type=MESH,
        )

    def right_copy(step):
        return pltpu.make_async_remote_copy(
            src_ref=right_all.at[row],
            dst_ref=right_all.at[row],
            send_sem=right_send_sem.at[step - 1],
            recv_sem=right_recv_sem.at[step - 1],
            device_id={"row": turn(outer, step, outers) * 2 + core},
            device_id_type=MESH,
        )

    def core_copy(step):
        source = turn(outer + outers, -step, outers) * 2 + core
        return pltpu.make_async_remote_copy(
            src_ref=right_all.at[source],
            dst_ref=right_all.at[source],
            send_sem=core_send_sem.at[step],
            recv_sem=core_recv_sem.at[step],
            device_id={"row": other_core},
            device_id_type=MESH,
        )

    def part_copy(q, step):
        return pltpu.make_async_remote_copy(
            src_ref=part_send.at[q, step - 1],
            dst_ref=part_recv.at[q, step - 1],
            send_sem=part_send_sem.at[q, step - 1],
            recv_sem=part_recv_sem.at[q, step - 1],
            device_id={"depth": turn(depth, step, n_depth)},
            device_id_type=MESH,
        )

    for step in range(1, outers):
        right_copy(step).start()
    for step in range(n_col - 1, 0, -1):
        left_copy(0, step).start()
    core_copy(0).start()
    for q in range(1, chunks):
        for step in range(n_col - 1, 0, -1):
            left_copy(q, step).start()

    left_slot = triples_ref[0:1, :]
    right_slot = triples_ref[1:2, :]
    out_slot = triples_ref[2:3, :]
    group_of = lax.rem(left_slot, groups)
    code = lax.div(left_slot, groups) * 1024 + lax.div(right_slot, groups)
    lane = lax.broadcasted_iota(jnp.int32, (16, width), 1)
    for k in range(0, PC, 16):
        here = out_slot == lax.broadcasted_iota(jnp.int32, (16, out_slot.shape[1]), 0) + k
        found = jnp.max(jnp.where(here, code, 0), axis=1, keepdims=True)
        code_rows[k : k + 16, :] = jnp.broadcast_to(found, (16, LANES))
        used = jnp.zeros((16, width), jnp.float32)
        for g in range(groups):
            at_group = jnp.max(
                jnp.where(here & (group_of == g), 1.0, 0.0).astype(jnp.float32), axis=1, keepdims=True
            )
            used = jnp.where(lane // order == g, at_group, used)
        mask_rows[k : k + 16, :] = used
    code_copy = pltpu.make_async_copy(code_rows, codes, code_sem)
    code_copy.start()

    def spread(k, carry):
        mask_ref[k] = jnp.broadcast_to(mask_rows[pl.ds(k, 1), :], (CHUNK_ROWS, width)).astype(jnp.bfloat16)
        return carry

    lax.fori_loop(0, PC, spread, 0, unroll=8)
    code_copy.wait()

    lower = lax.broadcasted_iota(jnp.int32, (order, LANES), 1) < order

    def split_right(shard):
        for j in range(local_rows // 2):
            for g in range(groups):
                rows = slice(g * order, (g + 1) * order)
                value = right_all[shard, j, rows, :]
                high = value.astype(jnp.bfloat16).astype(jnp.float32)
                low = pltpu.roll(value - high, order, 1)
                at = shard * local_rows + 2 * j
                right_split[at, rows, :] = jnp.where(lower, high, low).astype(jnp.bfloat16)
                right_split[at + 1, rows, :] = jnp.where(lower, low, high).astype(jnp.bfloat16)

    split_right(row)
    core_copy(0).wait_recv()
    split_right(other_core)
    for step in range(1, outers):
        right_copy(step).wait_recv()
        core_copy(step).start()
        split_right(turn(outer + outers, -step, outers) * 2 + core)
    for step in range(1, outers):
        core_copy(step).wait_recv()
        split_right(turn(outer + outers, -step, outers) * 2 + (1 - core))

    lane_low = lax.broadcasted_iota(jnp.int32, (CHUNK_ROWS, LANES), 1) < order

    def one_slot(q, k):
        found = codes[k, 0]
        picked = left_split[q, found // 1024]
        used = mask_ref[k]
        picked = picked * jnp.concatenate([used, used], axis=0)
        both = jnp.dot(picked, right_split[found % 1024], preferred_element_type=jnp.float32)
        both = both[:CHUNK_ROWS] + both[CHUNK_ROWS:]
        return both + pltpu.roll(both, order, 1)

    def products(q, first, target):
        def body(turn_index, carry):
            for inner in range(UNROLL_PAIRS):
                p = turn_index * UNROLL_PAIRS + inner
                k = first + 2 * p
                target[p] = jnp.where(lane_low, one_slot(q, k), one_slot(q, k + 1))
            return carry

        lax.fori_loop(0, pairs // UNROLL_PAIRS, body, 0)

    def finish(q):
        for step in range(1, n_depth):
            part_copy(q, step).wait_recv()

        def body(p, carry):
            total = part_own[q, p]
            for step in range(1, n_depth):
                total = total + part_recv[q, step - 1, p]
            rows = pl.ds(q * CHUNK_ROWS, CHUNK_ROWS)
            out_ref[2 * p, rows, :] = total[:, :order]
            out_ref[2 * p + 1, rows, :] = pltpu.roll(total, order, 1)[:, :order]
            return carry

        lax.fori_loop(0, pairs, body, 0, unroll=min(8, pairs))

    for q in range(chunks):
        for step in range(1, n_col):
            left_copy(q, step).wait_recv()
        for shard in range(n_col):
            for i in range(local_rows):
                high, low = split_bf16(left_all[q, shard, i])
                left_split[q, shard * local_rows + i, :CHUNK_ROWS, :] = high
                left_split[q, shard * local_rows + i, CHUNK_ROWS:, :] = low
        for step in range(1, n_depth):
            partner = turn(depth, step, n_depth)
            products(q, partner * share, part_send.at[q, step - 1])
            part_copy(q, step).start()
        products(q, depth * share, part_own.at[q])
        if q > 0:
            finish(q - 1)
    finish(chunks - 1)

    for q in range(chunks):
        for step in range(1, n_col):
            left_copy(q, step).wait_send()
        for step in range(1, n_depth):
            part_copy(q, step).wait_send()
    for step in range(1, outers):
        right_copy(step).wait_send()
    for step in range(outers):
        core_copy(step).wait_send()


def per_device(sizes, left_blocks, right_blocks, triples):
    n_row, n_col, n_depth, order, groups, local_rows, share, chunks = sizes
    width = groups * order
    pairs = share // 2
    f32, bf16, i32 = jnp.float32, jnp.bfloat16, jnp.int32
    dma = pltpu.SemaphoreType.DMA
    return pl.pallas_call(
        functools.partial(kernel, sizes),
        out_shape=jax.ShapeDtypeStruct((share, order, order), f32),
        in_specs=[pl.BlockSpec(memory_space=pltpu.VMEM)] * 3,
        out_specs=pl.BlockSpec(memory_space=pltpu.VMEM),
        scratch_shapes=[
            pltpu.VMEM((chunks, n_col, local_rows, CHUNK_ROWS, width), f32),
            pltpu.VMEM((n_row, local_rows // 2, width, LANES), f32),
            pltpu.VMEM((n_row * local_rows, width, LANES), bf16),
            pltpu.VMEM((chunks, n_col * local_rows, 2 * CHUNK_ROWS, width), bf16),
            pltpu.VMEM((PC, CHUNK_ROWS, width), bf16),
            pltpu.VMEM((PC, width), f32),
            pltpu.VMEM((PC, LANES), i32),
            pltpu.SMEM((PC, LANES), i32),
            pltpu.VMEM((chunks, n_depth - 1, pairs, CHUNK_ROWS, LANES), f32),
            pltpu.VMEM((chunks, n_depth - 1, pairs, CHUNK_ROWS, LANES), f32),
            pltpu.VMEM((chunks, pairs, CHUNK_ROWS, LANES), f32),
            dma((chunks, n_col - 1)),
            dma((chunks, n_col - 1)),
            dma((n_row // 2 - 1,)),
            dma((n_row // 2 - 1,)),
            dma((n_row // 2,)),
            dma((n_row // 2,)),
            dma((chunks, n_depth - 1)),
            dma((chunks, n_depth - 1)),
            dma(()),
        ],
        compiler_params=pltpu.CompilerParams(
            collective_id=0, has_side_effects=True, vmem_limit_bytes=48 * 1024 * 1024
        ),
        cost_estimate=pl.CostEstimate(
            flops=2 * PC * 4 * order * width * order, bytes_accessed=8 * 1024 * 1024, transcendentals=0
        ),
        name="filtered_product",
    )(left_blocks, right_blocks, triples)


def solution(mesh):
    n_row, n_col, n_depth = mesh.shape["row"], mesh.shape["col"], mesh.shape["depth"]
    devices = n_row * n_col * n_depth
    placed = (
        P(("row", "col", "depth"), None, None),
        P(("row", "col", "depth"), None, None),
        P(None, ("row", "col", "depth")),
    )

    def whole(left_blocks, right_blocks, triples):
        local = left_blocks.shape[0] // devices
        order = left_blocks.shape[1]
        groups = max(1, local // 4)
        sizes = (n_row, n_col, n_depth, order, groups, local // groups, PC // n_depth, order // CHUNK_ROWS)
        return jax.shard_map(
            functools.partial(per_device, sizes),
            mesh=mesh,
            in_specs=placed,
            out_specs=P(("row", "col", "depth"), None, None),
            check_vma=False,
        )(left_blocks, right_blocks, triples)

    return whole
```

```python
import functools

import jax
import jax.numpy as jnp
from jax import lax
from jax.experimental import pallas as pl
from jax.experimental.pallas import tpu as pltpu
from jax.sharding import PartitionSpec as P

PC = 128
LANES = 128
CHUNK_ROWS = 16
UNROLL_PAIRS = 4
HALVES = 2
MESH = pl.DeviceIdType.MESH


def split_bf16(value):
    high = value.astype(jnp.bfloat16)
    low = (value - high.astype(jnp.float32)).astype(jnp.bfloat16)
    return high, low


def kernel(
    sizes,
    left_hbm,
    right_hbm,
    triples_hbm,
    out_hbm,
    out_ref,
    left_ref,
    right_ref,
    triples_ref,
    left_all,
    right_all,
    right_split,
    left_split,
    mask_ref,
    mask_rows,
    code_rows,
    codes,
    part_send,
    part_recv,
    part_own,
    left_send_sem,
    left_recv_sem,
    right_send_sem,
    right_recv_sem,
    core_send_sem,
    core_recv_sem,
    part_send_sem,
    part_recv_sem,
    code_sem,
    in_sem,
    out_sem,
):
    n_row, n_col, n_depth, order, groups, local_rows, share, chunks = sizes
    row = lax.axis_index("row")
    col = lax.axis_index("col")
    depth = lax.axis_index("depth")
    outers = n_row // 2
    core = row % 2
    outer = row // 2
    other_core = outer * 2 + (1 - core)
    width = groups * order
    pairs = share // 2

    def turn(index, step, count):
        return lax.rem(index + step, count)

    fetches = [
        pltpu.make_async_copy(source, target, in_sem.at[n])
        for n, (source, target) in enumerate(
            ((right_hbm, right_ref), (left_hbm, left_ref), (triples_hbm, triples_ref))
        )
    ]
    for fetch in fetches:
        fetch.start()

    barrier = pltpu.get_barrier_semaphore()
    greeted = 0
    for step in range(1, n_col):
        pl.semaphore_signal(barrier, inc=1, device_id={"col": turn(col, step, n_col)}, device_id_type=MESH)
        greeted += 1
    for step in range(1, outers):
        pl.semaphore_signal(
            barrier, inc=1, device_id={"row": turn(outer, step, outers) * 2 + core}, device_id_type=MESH
        )
        greeted += 1
    pl.semaphore_signal(barrier, inc=1, device_id={"row": other_core}, device_id_type=MESH)
    greeted += 1
    for step in range(1, n_depth):
        pl.semaphore_signal(barrier, inc=1, device_id={"depth": turn(depth, step, n_depth)}, device_id_type=MESH)
        greeted += 1

    fetches[0].wait()
    for j in range(0, local_rows, 2):
        for g in range(groups):
            pair = jnp.concatenate([right_ref[j * groups + g], right_ref[(j + 1) * groups + g]], axis=-1)
            right_all[row, j // 2, g * order : (g + 1) * order, :] = pair
    fetches[1].wait()
    for i in range(local_rows):
        for g in range(0, groups, 2):
            pair = jnp.concatenate([left_ref[i * groups + g], left_ref[i * groups + g + 1]], axis=-1)
            for q in range(chunks):
                left_all[q, col, i, :, g * order : (g + 2) * order] = pair[q * CHUNK_ROWS : (q + 1) * CHUNK_ROWS]

    pl.semaphore_wait(barrier, greeted)

    def left_copy(q, step):
        return pltpu.make_async_remote_copy(
            src_ref=left_all.at[q, col],
            dst_ref=left_all.at[q, col],
            send_sem=left_send_sem.at[q, step - 1],
            recv_sem=left_recv_sem.at[q, step - 1],
            device_id={"col": turn(col, step, n_col)},
            device_id_type=MESH,
        )

    def right_copy(step):
        return pltpu.make_async_remote_copy(
            src_ref=right_all.at[row],
            dst_ref=right_all.at[row],
            send_sem=right_send_sem.at[step - 1],
            recv_sem=right_recv_sem.at[step - 1],
            device_id={"row": turn(outer, step, outers) * 2 + core},
            device_id_type=MESH,
        )

    def core_copy(step):
        source = turn(outer + outers, -step, outers) * 2 + core
        return pltpu.make_async_remote_copy(
            src_ref=right_all.at[source],
            dst_ref=right_all.at[source],
            send_sem=core_send_sem.at[step],
            recv_sem=core_recv_sem.at[step],
            device_id={"row": other_core},
            device_id_type=MESH,
        )

    def part_copy(q, step, half):
        piece = pl.ds(half * (pairs // HALVES), pairs // HALVES)
        return pltpu.make_async_remote_copy(
            src_ref=part_send.at[q, step - 1, piece],
            dst_ref=part_recv.at[q, step - 1, piece],
            send_sem=part_send_sem.at[q, step - 1, half],
            recv_sem=part_recv_sem.at[q, step - 1, half],
            device_id={"depth": turn(depth, step, n_depth)},
            device_id_type=MESH,
        )

    for step in range(1, outers):
        right_copy(step).start()
    for step in range(n_col - 1, 0, -1):
        left_copy(0, step).start()
    core_copy(0).start()
    for q in range(1, chunks):
        for step in range(n_col - 1, 0, -1):
            left_copy(q, step).start()

    fetches[2].wait()
    left_slot = triples_ref[0:1, :]
    right_slot = triples_ref[1:2, :]
    out_slot = triples_ref[2:3, :]
    group_of = lax.rem(left_slot, groups)
    block_row = lax.div(left_slot, groups)
    block_col = lax.div(right_slot, groups)
    code_lane = lax.broadcasted_iota(jnp.int32, (16, LANES), 1)
    lane = lax.broadcasted_iota(jnp.int32, (16, width), 1)
    for k in range(0, PC, 16):
        here = out_slot == lax.broadcasted_iota(jnp.int32, (16, out_slot.shape[1]), 0) + k
        at_row = jnp.max(jnp.where(here, block_row, 0), axis=1, keepdims=True)
        at_col = jnp.max(jnp.where(here, block_col, 0), axis=1, keepdims=True)
        code_rows[k : k + 16, :] = jnp.where(code_lane == 0, at_row, at_col)
        used = jnp.zeros((16, width), jnp.float32)
        for g in range(groups):
            at_group = jnp.max(
                jnp.where(here & (group_of == g), 1.0, 0.0).astype(jnp.float32), axis=1, keepdims=True
            )
            used = jnp.where(lane // order == g, at_group, used)
        mask_rows[k : k + 16, :] = used
    code_copy = pltpu.make_async_copy(code_rows, codes, code_sem)
    code_copy.start()

    def spread(k, carry):
        mask_ref[k] = jnp.broadcast_to(mask_rows[pl.ds(k, 1), :], (CHUNK_ROWS, width)).astype(jnp.bfloat16)
        return carry

    lax.fori_loop(0, PC, spread, 0, unroll=8)
    code_copy.wait()

    lower = lax.broadcasted_iota(jnp.int32, (order, LANES), 1) < order

    def split_right(shard):
        for j in range(local_rows // 2):
            for g in range(groups):
                rows = slice(g * order, (g + 1) * order)
                value = right_all[shard, j, rows, :]
                high = value.astype(jnp.bfloat16).astype(jnp.float32)
                low = pltpu.roll(value - high, order, 1)
                at = shard * local_rows + 2 * j
                right_split[at, rows, :] = jnp.where(lower, high, low).astype(jnp.bfloat16)
                right_split[at + 1, rows, :] = jnp.where(lower, low, high).astype(jnp.bfloat16)

    split_right(row)
    core_copy(0).wait_recv()
    split_right(other_core)
    for step in range(1, outers):
        right_copy(step).wait_recv()
        core_copy(step).start()
        split_right(turn(outer + outers, -step, outers) * 2 + core)
    for step in range(1, outers):
        core_copy(step).wait_recv()
        split_right(turn(outer + outers, -step, outers) * 2 + (1 - core))

    lane_low = lax.broadcasted_iota(jnp.int32, (CHUNK_ROWS, LANES), 1) < order

    def one_slot(q, k):
        picked = left_split[q, codes[k, 0]]
        used = mask_ref[k]
        picked = picked * jnp.concatenate([used, used], axis=0)
        both = jnp.dot(picked, right_split[codes[k, 1]], preferred_element_type=jnp.float32)
        both = both[:CHUNK_ROWS] + both[CHUNK_ROWS:]
        return both + pltpu.roll(both, order, 1)

    def products(q, first, target, half):
        def body(turn_index, carry):
            for inner in range(UNROLL_PAIRS):
                p = turn_index * UNROLL_PAIRS + inner
                k = first + 2 * p
                target[p] = jnp.where(lane_low, one_slot(q, k), one_slot(q, k + 1))
            return carry

        turns = pairs // UNROLL_PAIRS // HALVES
        lax.fori_loop(half * turns, (half + 1) * turns, body, 0)

    def out_copy(q):
        rows = pl.ds(q * CHUNK_ROWS, CHUNK_ROWS)
        return pltpu.make_async_copy(out_ref.at[:, rows, :], out_hbm.at[:, rows, :], out_sem.at[q])

    def finish(q):
        for step in range(1, n_depth):
            for half in range(HALVES):
                part_copy(q, step, half).wait_recv()

        def body(p, carry):
            total = part_own[q, p]
            for step in range(1, n_depth):
                total = total + part_recv[q, step - 1, p]
            rows = pl.ds(q * CHUNK_ROWS, CHUNK_ROWS)
            out_ref[2 * p, rows, :] = total[:, :order]
            out_ref[2 * p + 1, rows, :] = pltpu.roll(total, order, 1)[:, :order]
            return carry

        lax.fori_loop(0, pairs, body, 0, unroll=min(8, pairs))
        out_copy(q).start()

    for q in range(chunks):
        for step in range(1, n_col):
            left_copy(q, step).wait_recv()
        for shard in range(n_col):
            for i in range(local_rows):
                high, low = split_bf16(left_all[q, shard, i])
                left_split[q, shard * local_rows + i, :CHUNK_ROWS, :] = high
                left_split[q, shard * local_rows + i, CHUNK_ROWS:, :] = low
        for step in range(1, n_depth):
            partner = turn(depth, step, n_depth)
            for half in range(HALVES):
                products(q, partner * share, part_send.at[q, step - 1], half)
                part_copy(q, step, half).start()
        for half in range(HALVES):
            products(q, depth * share, part_own.at[q], half)
        if q > 0:
            finish(q - 1)
    finish(chunks - 1)

    for q in range(chunks):
        out_copy(q).wait()
        for step in range(1, n_col):
            left_copy(q, step).wait_send()
        for step in range(1, n_depth):
            for half in range(HALVES):
                part_copy(q, step, half).wait_send()
    for step in range(1, outers):
        right_copy(step).wait_send()
    for step in range(outers):
        core_copy(step).wait_send()


def per_device(sizes, left_blocks, right_blocks, triples):
    n_row, n_col, n_depth, order, groups, local_rows, share, chunks = sizes
    width = groups * order
    pairs = share // 2
    f32, bf16, i32 = jnp.float32, jnp.bfloat16, jnp.int32
    dma = pltpu.SemaphoreType.DMA
    return pl.pallas_call(
        functools.partial(kernel, sizes),
        out_shape=jax.ShapeDtypeStruct((share, order, order), f32),
        in_specs=[pl.BlockSpec(memory_space=pl.ANY)] * 3,
        out_specs=pl.BlockSpec(memory_space=pl.ANY),
        scratch_shapes=[
            pltpu.VMEM((share, order, order), f32),
            pltpu.VMEM(left_blocks.shape, f32),
            pltpu.VMEM(right_blocks.shape, f32),
            pltpu.VMEM(triples.shape, i32),
            pltpu.VMEM((chunks, n_col, local_rows, CHUNK_ROWS, width), f32),
            pltpu.VMEM((n_row, local_rows // 2, width, LANES), f32),
            pltpu.VMEM((n_row * local_rows, width, LANES), bf16),
            pltpu.VMEM((chunks, n_col * local_rows, 2 * CHUNK_ROWS, width), bf16),
            pltpu.VMEM((PC, CHUNK_ROWS, width), bf16),
            pltpu.VMEM((PC, width), f32),
            pltpu.VMEM((PC, LANES), i32),
            pltpu.SMEM((PC, LANES), i32),
            pltpu.VMEM((chunks, n_depth - 1, pairs, CHUNK_ROWS, LANES), f32),
            pltpu.VMEM((chunks, n_depth - 1, pairs, CHUNK_ROWS, LANES), f32),
            pltpu.VMEM((chunks, pairs, CHUNK_ROWS, LANES), f32),
            dma((chunks, n_col - 1)),
            dma((chunks, n_col - 1)),
            dma((n_row // 2 - 1,)),
            dma((n_row // 2 - 1,)),
            dma((n_row // 2,)),
            dma((n_row // 2,)),
            dma((chunks, n_depth - 1, HALVES)),
            dma((chunks, n_depth - 1, HALVES)),
            dma(()),
            dma((3,)),
            dma((chunks,)),
        ],
        compiler_params=pltpu.CompilerParams(
            collective_id=0, has_side_effects=True, vmem_limit_bytes=60 * 1024 * 1024
        ),
        cost_estimate=pl.CostEstimate(
            flops=2 * PC * 4 * order * width * order, bytes_accessed=8 * 1024 * 1024, transcendentals=0
        ),
        name="filtered_product",
    )(left_blocks, right_blocks, triples)


def solution(mesh):
    n_row, n_col, n_depth = mesh.shape["row"], mesh.shape["col"], mesh.shape["depth"]
    devices = n_row * n_col * n_depth
    placed = (
        P(("row", "col", "depth"), None, None),
        P(("row", "col", "depth"), None, None),
        P(None, ("row", "col", "depth")),
    )

    def whole(left_blocks, right_blocks, triples):
        local = left_blocks.shape[0] // devices
        order = left_blocks.shape[1]
        groups = max(1, local // 4)
        sizes = (n_row, n_col, n_depth, order, groups, local // groups, PC // n_depth, order // CHUNK_ROWS)
        return jax.shard_map(
            functools.partial(per_device, sizes),
            mesh=mesh,
            in_specs=placed,
            out_specs=P(("row", "col", "depth"), None, None),
            check_vma=False,
        )(left_blocks, right_blocks, triples)

    return whole
```

```python
import functools
import math

import jax
import jax.numpy as jnp
from jax import lax
from jax.experimental import pallas as pl
from jax.experimental.pallas import tpu as pltpu
from jax.sharding import PartitionSpec as P

PC = 128
LANES = 128
CHUNK_ROWS = 32
UNROLL_PAIRS = 4
HALVES = 2
MESH = pl.DeviceIdType.MESH


def split_bf16(value):
    high = value.astype(jnp.bfloat16)
    low = (value - high.astype(jnp.float32)).astype(jnp.bfloat16)
    return high, low


def kernel(
    sizes,
    left_hbm,
    right_hbm,
    triples_hbm,
    out_hbm,
    out_ref,
    left_ref,
    right_ref,
    triples_ref,
    left_all,
    right_all,
    right_split,
    left_split,
    mask_ref,
    mask_rows,
    code_rows,
    codes,
    part_send,
    part_recv,
    part_own,
    left_send_sem,
    left_recv_sem,
    right_send_sem,
    right_recv_sem,
    core_send_sem,
    core_recv_sem,
    part_send_sem,
    part_recv_sem,
    code_sem,
    in_sem,
    out_sem,
):
    n_row, n_col, n_depth, order, groups, local_rows, share, chunks = sizes
    row = lax.axis_index("row")
    col = lax.axis_index("col")
    depth = lax.axis_index("depth")
    outers = n_row // 2
    core = row % 2
    outer = row // 2
    other_core = outer * 2 + (1 - core)
    width = groups * order
    pairs = share // 2

    def turn(index, step, count):
        return lax.rem(index + step, count)

    fetches = [
        pltpu.make_async_copy(source, target, in_sem.at[n])
        for n, (source, target) in enumerate(
            ((right_hbm, right_ref), (left_hbm, left_ref), (triples_hbm, triples_ref))
        )
    ]
    for fetch in fetches:
        fetch.start()

    barrier = pltpu.get_barrier_semaphore()
    greeted = 0
    for step in range(1, n_col):
        pl.semaphore_signal(barrier, inc=1, device_id={"col": turn(col, step, n_col)}, device_id_type=MESH)
        greeted += 1
    for step in range(1, outers):
        pl.semaphore_signal(
            barrier, inc=1, device_id={"row": turn(outer, step, outers) * 2 + core}, device_id_type=MESH
        )
        greeted += 1
    pl.semaphore_signal(barrier, inc=1, device_id={"row": other_core}, device_id_type=MESH)
    greeted += 1
    for step in range(1, n_depth):
        pl.semaphore_signal(barrier, inc=1, device_id={"depth": turn(depth, step, n_depth)}, device_id_type=MESH)
        greeted += 1

    fetches[0].wait()
    for j in range(0, local_rows, 2):
        for g in range(groups):
            pair = jnp.concatenate([right_ref[j * groups + g], right_ref[(j + 1) * groups + g]], axis=-1)
            right_all[row, j // 2, g * order : (g + 1) * order, :] = pair
    fetches[1].wait()
    for i in range(local_rows):
        for g in range(0, groups, 2):
            pair = jnp.concatenate([left_ref[i * groups + g], left_ref[i * groups + g + 1]], axis=-1)
            for q in range(chunks):
                left_all[q, col, i, :, g * order : (g + 2) * order] = pair[q * CHUNK_ROWS : (q + 1) * CHUNK_ROWS]

    pl.semaphore_wait(barrier, greeted)

    def left_copy(q, step):
        return pltpu.make_async_remote_copy(
            src_ref=left_all.at[q, col],
            dst_ref=left_all.at[q, col],
            send_sem=left_send_sem.at[q, step - 1],
            recv_sem=left_recv_sem.at[q, step - 1],
            device_id={"col": turn(col, step, n_col)},
            device_id_type=MESH,
        )

    def right_copy(step):
        return pltpu.make_async_remote_copy(
            src_ref=right_all.at[row],
            dst_ref=right_all.at[row],
            send_sem=right_send_sem.at[step - 1],
            recv_sem=right_recv_sem.at[step - 1],
            device_id={"row": turn(outer, step, outers) * 2 + core},
            device_id_type=MESH,
        )

    def core_copy(step):
        source = turn(outer + outers, -step, outers) * 2 + core
        return pltpu.make_async_remote_copy(
            src_ref=right_all.at[source],
            dst_ref=right_all.at[source],
            send_sem=core_send_sem.at[step],
            recv_sem=core_recv_sem.at[step],
            device_id={"row": other_core},
            device_id_type=MESH,
        )

    def part_copy(q, step, half):
        piece = pl.ds(half * (pairs // HALVES), pairs // HALVES)
        return pltpu.make_async_remote_copy(
            src_ref=part_send.at[q, step - 1, piece],
            dst_ref=part_recv.at[q, step - 1, piece],
            send_sem=part_send_sem.at[q, step - 1, half],
            recv_sem=part_recv_sem.at[q, step - 1, half],
            device_id={"depth": turn(depth, step, n_depth)},
            device_id_type=MESH,
        )

    for step in range(1, outers):
        right_copy(step).start()
    for step in range(n_col - 1, 0, -1):
        left_copy(0, step).start()
    core_copy(0).start()
    for q in range(1, chunks):
        for step in range(n_col - 1, 0, -1):
            left_copy(q, step).start()

    fetches[2].wait()
    left_slot = triples_ref[0:1, :]
    right_slot = triples_ref[1:2, :]
    out_slot = triples_ref[2:3, :]
    group_of = lax.rem(left_slot, groups)
    block_row = lax.div(left_slot, groups)
    block_col = lax.div(right_slot, groups)
    code_lane = lax.broadcasted_iota(jnp.int32, (16, LANES), 1)
    lane = lax.broadcasted_iota(jnp.int32, (16, width), 1)
    for k in range(0, PC, 16):
        here = out_slot == lax.broadcasted_iota(jnp.int32, (16, out_slot.shape[1]), 0) + k
        at_row = jnp.max(jnp.where(here, block_row, 0), axis=1, keepdims=True)
        at_col = jnp.max(jnp.where(here, block_col, 0), axis=1, keepdims=True)
        code_rows[k : k + 16, :] = jnp.where(code_lane == 0, at_row, at_col)
        used = jnp.zeros((16, width), jnp.float32)
        for g in range(groups):
            at_group = jnp.max(
                jnp.where(here & (group_of == g), 1.0, 0.0).astype(jnp.float32), axis=1, keepdims=True
            )
            used = jnp.where(lane // order == g, at_group, used)
        mask_rows[k : k + 16, :] = used
    code_copy = pltpu.make_async_copy(code_rows, codes, code_sem)
    code_copy.start()

    def spread(k, carry):
        mask_ref[k] = jnp.broadcast_to(mask_rows[pl.ds(k, 1), :], (CHUNK_ROWS, width)).astype(jnp.bfloat16)
        return carry

    lax.fori_loop(0, PC, spread, 0, unroll=8)
    code_copy.wait()

    lower = lax.broadcasted_iota(jnp.int32, (order, LANES), 1) < order

    def split_right(shard):
        for j in range(local_rows // 2):
            for g in range(groups):
                rows = slice(g * order, (g + 1) * order)
                value = right_all[shard, j, rows, :]
                high = value.astype(jnp.bfloat16).astype(jnp.float32)
                low = pltpu.roll(value - high, order, 1)
                at = shard * local_rows + 2 * j
                right_split[at, rows, :] = jnp.where(lower, high, low).astype(jnp.bfloat16)
                right_split[at + 1, rows, :] = jnp.where(lower, low, high).astype(jnp.bfloat16)

    split_right(row)
    core_copy(0).wait_recv()
    split_right(other_core)
    for step in range(1, outers):
        right_copy(step).wait_recv()
        core_copy(step).start()
        split_right(turn(outer + outers, -step, outers) * 2 + core)
    for step in range(1, outers):
        core_copy(step).wait_recv()
        split_right(turn(outer + outers, -step, outers) * 2 + (1 - core))

    lane_low = lax.broadcasted_iota(jnp.int32, (CHUNK_ROWS, LANES), 1) < order

    def one_slot(q, k):
        picked = left_split[q, codes[k, 0]]
        used = mask_ref[k]
        picked = picked * jnp.concatenate([used, used], axis=0)
        both = jnp.dot(picked, right_split[codes[k, 1]], preferred_element_type=jnp.float32)
        both = both[:CHUNK_ROWS] + both[CHUNK_ROWS:]
        return both + pltpu.roll(both, order, 1)

    def products(q, first, target, half):
        def body(turn_index, carry):
            for inner in range(UNROLL_PAIRS):
                p = turn_index * UNROLL_PAIRS + inner
                k = first + 2 * p
                target[p] = jnp.where(lane_low, one_slot(q, k), one_slot(q, k + 1))
            return carry

        turns = pairs // UNROLL_PAIRS // HALVES
        lax.fori_loop(half * turns, (half + 1) * turns, body, 0)

    def out_copy(q):
        rows = pl.ds(q * CHUNK_ROWS, CHUNK_ROWS)
        return pltpu.make_async_copy(out_ref.at[:, rows, :], out_hbm.at[:, rows, :], out_sem.at[q])

    def finish(q):
        for step in range(1, n_depth):
            for half in range(HALVES):
                part_copy(q, step, half).wait_recv()

        def body(p, carry):
            total = part_own[q, p]
            for step in range(1, n_depth):
                total = total + part_recv[q, step - 1, p]
            rows = pl.ds(q * CHUNK_ROWS, CHUNK_ROWS)
            out_ref[p, rows, :] = total
            return carry

        lax.fori_loop(0, pairs, body, 0, unroll=min(8, pairs))
        out_copy(q).start()

    for q in range(chunks):
        for step in range(1, n_col):
            left_copy(q, step).wait_recv()
        for shard in range(n_col):
            for i in range(local_rows):
                high, low = split_bf16(left_all[q, shard, i])
                left_split[q, shard * local_rows + i, :CHUNK_ROWS, :] = high
                left_split[q, shard * local_rows + i, CHUNK_ROWS:, :] = low
        for step in range(1, n_depth):
            partner = turn(depth, step, n_depth)
            for half in range(HALVES):
                products(q, partner * share, part_send.at[q, step - 1], half)
                part_copy(q, step, half).start()
        for half in range(HALVES):
            products(q, depth * share, part_own.at[q], half)
        if q > 0:
            finish(q - 1)
    finish(chunks - 1)

    for q in range(chunks):
        out_copy(q).wait()
        for step in range(1, n_col):
            left_copy(q, step).wait_send()
        for step in range(1, n_depth):
            for half in range(HALVES):
                part_copy(q, step, half).wait_send()
    for step in range(1, outers):
        right_copy(step).wait_send()
    for step in range(outers):
        core_copy(step).wait_send()


def unpack(packed_ref, kept_ref):
    order = kept_ref.shape[1]
    for p in range(packed_ref.shape[0]):
        pair = packed_ref[p]
        kept_ref[2 * p] = pair[:, :order]
        kept_ref[2 * p + 1] = pltpu.roll(pair, order, 1)[:, :order]


def per_device(sizes, left_blocks, right_blocks, triples):
    n_row, n_col, n_depth, order, groups, local_rows, share, chunks = sizes
    width = groups * order
    pairs = share // 2
    f32, bf16, i32 = jnp.float32, jnp.bfloat16, jnp.int32
    dma = pltpu.SemaphoreType.DMA
    packed = pl.pallas_call(
        functools.partial(kernel, sizes),
        out_shape=jax.ShapeDtypeStruct((pairs, order, LANES), f32),
        in_specs=[pl.BlockSpec(memory_space=pl.ANY)] * 3,
        out_specs=pl.BlockSpec(memory_space=pl.ANY),
        scratch_shapes=[
            pltpu.VMEM((pairs, order, LANES), f32),
            pltpu.VMEM(left_blocks.shape, f32),
            pltpu.VMEM(right_blocks.shape, f32),
            pltpu.VMEM(triples.shape, i32),
            pltpu.VMEM((chunks, n_col, local_rows, CHUNK_ROWS, width), f32),
            pltpu.VMEM((n_row, local_rows // 2, width, LANES), f32),
            pltpu.VMEM((n_row * local_rows, width, LANES), bf16),
            pltpu.VMEM((chunks, n_col * local_rows, 2 * CHUNK_ROWS, width), bf16),
            pltpu.VMEM((PC, CHUNK_ROWS, width), bf16),
            pltpu.VMEM((PC, width), f32),
            pltpu.VMEM((PC, LANES), i32),
            pltpu.SMEM((PC, LANES), i32),
            pltpu.VMEM((chunks, n_depth - 1, pairs, CHUNK_ROWS, LANES), f32),
            pltpu.VMEM((chunks, n_depth - 1, pairs, CHUNK_ROWS, LANES), f32),
            pltpu.VMEM((chunks, pairs, CHUNK_ROWS, LANES), f32),
            dma((chunks, n_col - 1)),
            dma((chunks, n_col - 1)),
            dma((n_row // 2 - 1,)),
            dma((n_row // 2 - 1,)),
            dma((n_row // 2,)),
            dma((n_row // 2,)),
            dma((chunks, n_depth - 1, HALVES)),
            dma((chunks, n_depth - 1, HALVES)),
            dma(()),
            dma((3,)),
            dma((chunks,)),
        ],
        compiler_params=pltpu.CompilerParams(
            collective_id=0, has_side_effects=True, vmem_limit_bytes=60 * 1024 * 1024
        ),
        cost_estimate=pl.CostEstimate(
            flops=2 * PC * 4 * order * width * order, bytes_accessed=8 * 1024 * 1024, transcendentals=0
        ),
        name="filtered_product",
    )(left_blocks, right_blocks, triples)
    steps = math.gcd(pairs, 4)
    return pl.pallas_call(
        unpack,
        out_shape=jax.ShapeDtypeStruct((share, order, order), f32),
        grid=(steps,),
        in_specs=[pl.BlockSpec((pairs // steps, order, LANES), lambda n: (n, 0, 0))],
        out_specs=pl.BlockSpec((share // steps, order, order), lambda n: (n, 0, 0)),
        name="unpack_blocks",
    )(packed)


def solution(mesh):
    n_row, n_col, n_depth = mesh.shape["row"], mesh.shape["col"], mesh.shape["depth"]
    devices = n_row * n_col * n_depth
    placed = (
        P(("row", "col", "depth"), None, None),
        P(("row", "col", "depth"), None, None),
        P(None, ("row", "col", "depth")),
    )

    def whole(left_blocks, right_blocks, triples):
        local = left_blocks.shape[0] // devices
        order = left_blocks.shape[1]
        groups = max(1, local // 4)
        sizes = (n_row, n_col, n_depth, order, groups, local // groups, PC // n_depth, order // CHUNK_ROWS)
        return jax.shard_map(
            functools.partial(per_device, sizes),
            mesh=mesh,
            in_specs=placed,
            out_specs=P(("row", "col", "depth"), None, None),
            check_vma=False,
        )(left_blocks, right_blocks, triples)

    return whole
```

```python
import functools

import jax
import jax.numpy as jnp
from jax import lax
from jax.experimental import pallas as pl
from jax.experimental.pallas import tpu as pltpu
from jax.sharding import PartitionSpec as P

PC = 128
LANES = 128
CHUNK_ROWS = 16
UNROLL_PAIRS = 4
HALVES = 2
MESH = pl.DeviceIdType.MESH


def split_bf16(value):
    high = value.astype(jnp.bfloat16)
    low = (value - high.astype(jnp.float32)).astype(jnp.bfloat16)
    return high, low


def kernel(
    sizes,
    left_hbm,
    right_hbm,
    triples_hbm,
    out_ref,
    left_ref,
    right_ref,
    triples_ref,
    left_all,
    right_all,
    right_split,
    left_split,
    mask_ref,
    mask_rows,
    code_rows,
    codes,
    part_send,
    part_recv,
    part_own,
    left_send_sem,
    left_recv_sem,
    right_send_sem,
    right_recv_sem,
    core_send_sem,
    core_recv_sem,
    part_send_sem,
    part_recv_sem,
    code_sem,
    in_sem,
):
    n_row, n_col, n_depth, order, groups, local_rows, share, chunks = sizes
    row = lax.axis_index("row")
    col = lax.axis_index("col")
    depth = lax.axis_index("depth")
    outers = n_row // 2
    core = row % 2
    outer = row // 2
    other_core = outer * 2 + (1 - core)
    width = groups * order
    pairs = share // 2

    def turn(index, step, count):
        return lax.rem(index + step, count)

    fetches = [
        pltpu.make_async_copy(source, target, in_sem.at[n])
        for n, (source, target) in enumerate(
            ((right_hbm, right_ref), (left_hbm, left_ref), (triples_hbm, triples_ref))
        )
    ]
    for fetch in fetches:
        fetch.start()

    barrier = pltpu.get_barrier_semaphore()
    greeted = 0
    for step in range(1, n_col):
        pl.semaphore_signal(barrier, inc=1, device_id={"col": turn(col, step, n_col)}, device_id_type=MESH)
        greeted += 1
    for step in range(1, outers):
        pl.semaphore_signal(
            barrier, inc=1, device_id={"row": turn(outer, step, outers) * 2 + core}, device_id_type=MESH
        )
        greeted += 1
    pl.semaphore_signal(barrier, inc=1, device_id={"row": other_core}, device_id_type=MESH)
    greeted += 1
    for step in range(1, n_depth):
        pl.semaphore_signal(barrier, inc=1, device_id={"depth": turn(depth, step, n_depth)}, device_id_type=MESH)
        greeted += 1

    fetches[0].wait()
    for j in range(0, local_rows, 2):
        for g in range(groups):
            pair = jnp.concatenate([right_ref[j * groups + g], right_ref[(j + 1) * groups + g]], axis=-1)
            right_all[row, j // 2, g * order : (g + 1) * order, :] = pair
    fetches[1].wait()
    for i in range(local_rows):
        for g in range(0, groups, 2):
            pair = jnp.concatenate([left_ref[i * groups + g], left_ref[i * groups + g + 1]], axis=-1)
            for q in range(chunks):
                left_all[q, col, i, :, g * order : (g + 2) * order] = pair[q * CHUNK_ROWS : (q + 1) * CHUNK_ROWS]

    pl.semaphore_wait(barrier, greeted)

    def left_copy(q, shard, way, hops):
        return pltpu.make_async_remote_copy(
            src_ref=left_all.at[q, shard],
            dst_ref=left_all.at[q, shard],
            send_sem=left_send_sem.at[q, max(way, 0), hops],
            recv_sem=left_recv_sem.at[q, max(way, 0), hops],
            device_id={"col": turn(col + n_col, way, n_col)},
            device_id_type=MESH,
        )

    def along(way, hops, act):
        shard = col - way * hops
        ahead = col + way
        held = jnp.logical_and(shard >= 0, shard < n_col)

        @pl.when(jnp.logical_and(held, jnp.logical_and(ahead >= 0, ahead < n_col)))
        def _():
            act(shard)

    def left_start(q, hops):
        for way in (1, -1):
            along(way, hops, lambda shard: left_copy(q, shard, way, hops).start())

    def left_arrive(q, hops):
        for way in (1, -1):
            shard = col - way * hops

            @pl.when(jnp.logical_and(shard >= 0, shard < n_col))
            def _():
                left_copy(q, shard, way, hops - 1).wait_recv()

            along(way, hops, lambda shard: left_copy(q, shard, way, hops).start())

    def right_copy(step):
        return pltpu.make_async_remote_copy(
            src_ref=right_all.at[row],
            dst_ref=right_all.at[row],
            send_sem=right_send_sem.at[step - 1],
            recv_sem=right_recv_sem.at[step - 1],
            device_id={"row": turn(outer, step, outers) * 2 + core},
            device_id_type=MESH,
        )

    def core_copy(step):
        source = turn(outer + outers, -step, outers) * 2 + core
        return pltpu.make_async_remote_copy(
            src_ref=right_all.at[source],
            dst_ref=right_all.at[source],
            send_sem=core_send_sem.at[step],
            recv_sem=core_recv_sem.at[step],
            device_id={"row": other_core},
            device_id_type=MESH,
        )

    def part_copy(q, step, half):
        piece = pl.ds(half * (pairs // HALVES), pairs // HALVES)
        return pltpu.make_async_remote_copy(
            src_ref=part_send.at[q, step - 1, piece],
            dst_ref=part_recv.at[q, step - 1, piece],
            send_sem=part_send_sem.at[q, step - 1, half],
            recv_sem=part_recv_sem.at[q, step - 1, half],
            device_id={"depth": turn(depth, step, n_depth)},
            device_id_type=MESH,
        )

    for step in range(1, outers):
        right_copy(step).start()
    left_start(0, 0)
    core_copy(0).start()
    if chunks > 1:
        left_start(1, 0)

    fetches[2].wait()
    left_slot = triples_ref[0:1, :]
    right_slot = triples_ref[1:2, :]
    out_slot = triples_ref[2:3, :]
    group_of = lax.rem(left_slot, groups)
    block_row = lax.div(left_slot, groups)
    block_col = lax.div(right_slot, groups)
    code_lane = lax.broadcasted_iota(jnp.int32, (16, LANES), 1)
    lane = lax.broadcasted_iota(jnp.int32, (16, width), 1)
    for k in range(0, PC, 16):
        here = out_slot == lax.broadcasted_iota(jnp.int32, (16, out_slot.shape[1]), 0) + k
        at_row = jnp.max(jnp.where(here, block_row, 0), axis=1, keepdims=True)
        at_col = jnp.max(jnp.where(here, block_col, 0), axis=1, keepdims=True)
        code_rows[k : k + 16, :] = jnp.where(code_lane == 0, at_row, at_col)
        used = jnp.zeros((16, width), jnp.float32)
        for g in range(groups):
            at_group = jnp.max(
                jnp.where(here & (group_of == g), 1.0, 0.0).astype(jnp.float32), axis=1, keepdims=True
            )
            used = jnp.where(lane // order == g, at_group, used)
        mask_rows[k : k + 16, :] = used
    code_copy = pltpu.make_async_copy(code_rows, codes, code_sem)
    code_copy.start()

    def spread(k, carry):
        mask_ref[k] = jnp.broadcast_to(mask_rows[pl.ds(k, 1), :], (CHUNK_ROWS, width)).astype(jnp.bfloat16)
        return carry

    lax.fori_loop(0, PC, spread, 0, unroll=8)
    code_copy.wait()

    lower = lax.broadcasted_iota(jnp.int32, (order, LANES), 1) < order

    def split_right(shard):
        for j in range(local_rows // 2):
            for g in range(groups):
                rows = slice(g * order, (g + 1) * order)
                value = right_all[shard, j, rows, :]
                high = value.astype(jnp.bfloat16).astype(jnp.float32)
                low = pltpu.roll(value - high, order, 1)
                at = shard * local_rows + 2 * j
                right_split[at, rows, :] = jnp.where(lower, high, low).astype(jnp.bfloat16)
                right_split[at + 1, rows, :] = jnp.where(lower, low, high).astype(jnp.bfloat16)

    for hops in range(1, n_col - 1):
        left_arrive(0, hops)
    split_right(row)
    core_copy(0).wait_recv()
    split_right(other_core)
    for step in range(1, outers):
        right_copy(step).wait_recv()
        core_copy(step).start()
        split_right(turn(outer + outers, -step, outers) * 2 + core)
    for step in range(1, outers):
        core_copy(step).wait_recv()
        split_right(turn(outer + outers, -step, outers) * 2 + (1 - core))

    lane_low = lax.broadcasted_iota(jnp.int32, (CHUNK_ROWS, LANES), 1) < order

    def one_slot(q, k):
        picked = left_split[q, codes[k, 0]]
        used = mask_ref[k]
        picked = picked * jnp.concatenate([used, used], axis=0)
        both = jnp.dot(picked, right_split[codes[k, 1]], preferred_element_type=jnp.float32)
        both = both[:CHUNK_ROWS] + both[CHUNK_ROWS:]
        return both + pltpu.roll(both, order, 1)

    def products(q, first, target, half):
        def body(turn_index, carry):
            for inner in range(UNROLL_PAIRS):
                p = turn_index * UNROLL_PAIRS + inner
                k = first + 2 * p
                target[p] = jnp.where(lane_low, one_slot(q, k), one_slot(q, k + 1))
            return carry

        turns = pairs // UNROLL_PAIRS // HALVES
        lax.fori_loop(half * turns, (half + 1) * turns, body, 0)

    def finish(q):
        for step in range(1, n_depth):
            for half in range(HALVES):
                part_copy(q, step, half).wait_recv()

        def body(p, carry):
            total = part_own[q, p]
            for step in range(1, n_depth):
                total = total + part_recv[q, step - 1, p]
            rows = pl.ds(q * CHUNK_ROWS, CHUNK_ROWS)
            out_ref[2 * p, rows, :] = total[:, :order]
            out_ref[2 * p + 1, rows, :] = pltpu.roll(total, order, 1)[:, :order]
            return carry

        lax.fori_loop(0, pairs, body, 0, unroll=min(8, pairs))

    for q in range(chunks):
        left_arrive(q, n_col - 1)
        if q + 2 < chunks:
            left_start(q + 2, 0)
        for shard in range(n_col):
            for i in range(local_rows):
                high, low = split_bf16(left_all[q, shard, i])
                left_split[q, shard * local_rows + i, :CHUNK_ROWS, :] = high
                left_split[q, shard * local_rows + i, CHUNK_ROWS:, :] = low
        for step in range(1, n_depth):
            partner = turn(depth, step, n_depth)
            for half in range(HALVES):
                products(q, partner * share, part_send.at[q, step - 1], half)
                part_copy(q, step, half).start()
        hops_ahead = range(1, n_col - 1) if q + 1 < chunks else range(0)
        for half in range(HALVES):
            for hops in hops_ahead[half::HALVES]:
                left_arrive(q + 1, hops)
            products(q, depth * share, part_own.at[q], half)
        if q > 0:
            finish(q - 1)
    finish(chunks - 1)

    for q in range(chunks):
        for hops in range(n_col - 1):
            for way in (1, -1):
                along(way, hops, lambda shard: left_copy(q, shard, way, hops).wait_send())
        for step in range(1, n_depth):
            for half in range(HALVES):
                part_copy(q, step, half).wait_send()
    for step in range(1, outers):
        right_copy(step).wait_send()
    for step in range(outers):
        core_copy(step).wait_send()


def per_device(sizes, left_blocks, right_blocks, triples):
    n_row, n_col, n_depth, order, groups, local_rows, share, chunks = sizes
    width = groups * order
    pairs = share // 2
    f32, bf16, i32 = jnp.float32, jnp.bfloat16, jnp.int32
    dma = pltpu.SemaphoreType.DMA
    return pl.pallas_call(
        functools.partial(kernel, sizes),
        out_shape=jax.ShapeDtypeStruct((share, order, order), f32),
        in_specs=[pl.BlockSpec(memory_space=pl.ANY)] * 3,
        out_specs=pl.BlockSpec(memory_space=pltpu.VMEM),
        scratch_shapes=[
            pltpu.VMEM(left_blocks.shape, f32),
            pltpu.VMEM(right_blocks.shape, f32),
            pltpu.VMEM(triples.shape, i32),
            pltpu.VMEM((chunks, n_col, local_rows, CHUNK_ROWS, width), f32),
            pltpu.VMEM((n_row, local_rows // 2, width, LANES), f32),
            pltpu.VMEM((n_row * local_rows, width, LANES), bf16),
            pltpu.VMEM((chunks, n_col * local_rows, 2 * CHUNK_ROWS, width), bf16),
            pltpu.VMEM((PC, CHUNK_ROWS, width), bf16),
            pltpu.VMEM((PC, width), f32),
            pltpu.VMEM((PC, LANES), i32),
            pltpu.SMEM((PC, LANES), i32),
            pltpu.VMEM((chunks, n_depth - 1, pairs, CHUNK_ROWS, LANES), f32),
            pltpu.VMEM((chunks, n_depth - 1, pairs, CHUNK_ROWS, LANES), f32),
            pltpu.VMEM((chunks, pairs, CHUNK_ROWS, LANES), f32),
            dma((chunks, 2, n_col - 1)),
            dma((chunks, 2, n_col - 1)),
            dma((n_row // 2 - 1,)),
            dma((n_row // 2 - 1,)),
            dma((n_row // 2,)),
            dma((n_row // 2,)),
            dma((chunks, n_depth - 1, HALVES)),
            dma((chunks, n_depth - 1, HALVES)),
            dma(()),
            dma((3,)),
        ],
        compiler_params=pltpu.CompilerParams(
            collective_id=0, has_side_effects=True, vmem_limit_bytes=48 * 1024 * 1024
        ),
        cost_estimate=pl.CostEstimate(
            flops=2 * PC * 4 * order * width * order, bytes_accessed=8 * 1024 * 1024, transcendentals=0
        ),
        name="filtered_product",
    )(*(pltpu.with_memory_space_constraint(x, pltpu.HBM) for x in (left_blocks, right_blocks, triples)))


def solution(mesh):
    n_row, n_col, n_depth = mesh.shape["row"], mesh.shape["col"], mesh.shape["depth"]
    devices = n_row * n_col * n_depth
    placed = (
        P(("row", "col", "depth"), None, None),
        P(("row", "col", "depth"), None, None),
        P(None, ("row", "col", "depth")),
    )

    def whole(left_blocks, right_blocks, triples):
        local = left_blocks.shape[0] // devices
        order = left_blocks.shape[1]
        groups = max(1, local // 4)
        sizes = (n_row, n_col, n_depth, order, groups, local // groups, PC // n_depth, order // CHUNK_ROWS)
        return jax.shard_map(
            functools.partial(per_device, sizes),
            mesh=mesh,
            in_specs=placed,
            out_specs=P(("row", "col", "depth"), None, None),
            check_vma=False,
        )(left_blocks, right_blocks, triples)

    return whole
```

```python
import functools

import jax
import jax.numpy as jnp
from jax import lax
from jax.experimental import pallas as pl
from jax.experimental.pallas import tpu as pltpu
from jax.sharding import PartitionSpec as P

PC = 128
LANES = 128
CHUNK_ROWS = 16
UNROLL_PAIRS = 4
HALVES = 2
HYBRID = 1
MESH = pl.DeviceIdType.MESH


def split_bf16(value):
    high = value.astype(jnp.bfloat16)
    low = (value - high.astype(jnp.float32)).astype(jnp.bfloat16)
    return high, low


def kernel(
    sizes,
    left_hbm,
    right_hbm,
    triples_hbm,
    out_ref,
    left_ref,
    right_ref,
    triples_both,
    left_all,
    right_all,
    right_split,
    left_split,
    mask_ref,
    mask_rows,
    code_rows,
    codes,
    part_send,
    part_recv,
    part_own,
    left_send_sem,
    left_recv_sem,
    right_send_sem,
    right_recv_sem,
    core_send_sem,
    core_recv_sem,
    part_send_sem,
    part_recv_sem,
    code_sem,
    in_sem,
    layer_send_sem,
    layer_recv_sem,
):
    n_row, n_col, n_depth, order, groups, local_rows, share, chunks, hybrid = sizes
    row = lax.axis_index("row")
    col = lax.axis_index("col")
    depth = lax.axis_index("depth")
    outers = n_row // 2
    core = row % 2
    outer = row // 2
    other_core = outer * 2 + (1 - core)
    width = groups * order
    pairs = share // 2

    def turn(index, step, count):
        return lax.rem(index + step, count)

    fetches = [
        pltpu.make_async_copy(source, target, in_sem.at[n])
        for n, (source, target) in enumerate(
            ((right_hbm, right_ref), (left_hbm, left_ref), (triples_hbm, triples_both.at[0]))
        )
    ]
    for fetch in fetches:
        fetch.start()

    barrier = pltpu.get_barrier_semaphore()
    greeted = 0
    for step in range(1, n_col):
        pl.semaphore_signal(barrier, inc=1, device_id={"col": turn(col, step, n_col)}, device_id_type=MESH)
        greeted += 1
    for step in range(1, outers):
        pl.semaphore_signal(
            barrier, inc=1, device_id={"row": turn(outer, step, outers) * 2 + core}, device_id_type=MESH
        )
        greeted += 1
    pl.semaphore_signal(barrier, inc=1, device_id={"row": other_core}, device_id_type=MESH)
    greeted += 1
    for step in range(1, n_depth):
        pl.semaphore_signal(barrier, inc=1, device_id={"depth": turn(depth, step, n_depth)}, device_id_type=MESH)
        greeted += 1

    fetches[0].wait()
    for j in range(0, local_rows, 2):
        for g in range(groups):
            pair = jnp.concatenate([right_ref[j * groups + g], right_ref[(j + 1) * groups + g]], axis=-1)
            right_all[0, row, j // 2, g * order : (g + 1) * order, :] = pair
    fetches[1].wait()
    for i in range(local_rows):
        for g in range(0, groups, 2):
            pair = jnp.concatenate([left_ref[i * groups + g], left_ref[i * groups + g + 1]], axis=-1)
            for q in range(chunks):
                left_all[q, col, i, :, g * order : (g + 2) * order] = pair[q * CHUNK_ROWS : (q + 1) * CHUNK_ROWS]

    pl.semaphore_wait(barrier, greeted)

    def left_copy(q, shard, way, hops):
        return pltpu.make_async_remote_copy(
            src_ref=left_all.at[q, shard],
            dst_ref=left_all.at[q, shard],
            send_sem=left_send_sem.at[q, max(way, 0), hops],
            recv_sem=left_recv_sem.at[q, max(way, 0), hops],
            device_id={"col": turn(col + n_col, way, n_col)},
            device_id_type=MESH,
        )

    def along(way, hops, act):
        shard = col - way * hops
        ahead = col + way
        held = jnp.logical_and(shard >= 0, shard < n_col)

        @pl.when(jnp.logical_and(held, jnp.logical_and(ahead >= 0, ahead < n_col)))
        def _():
            act(shard)

    def left_start(q, hops):
        for way in (1, -1):
            along(way, hops, lambda shard: left_copy(q, shard, way, hops).start())

    def left_arrive(q, hops):
        for way in (1, -1):
            shard = col - way * hops

            @pl.when(jnp.logical_and(shard >= 0, shard < n_col))
            def _():
                left_copy(q, shard, way, hops - 1).wait_recv()

            along(way, hops, lambda shard: left_copy(q, shard, way, hops).start())

    def right_copy(layer, step):
        return pltpu.make_async_remote_copy(
            src_ref=right_all.at[layer, row],
            dst_ref=right_all.at[layer, row],
            send_sem=right_send_sem.at[layer, step - 1],
            recv_sem=right_recv_sem.at[layer, step - 1],
            device_id={"row": turn(outer, step, outers) * 2 + core},
            device_id_type=MESH,
        )

    def core_copy(layer, step):
        source = turn(outer + outers, -step, outers) * 2 + core
        return pltpu.make_async_remote_copy(
            src_ref=right_all.at[layer, source],
            dst_ref=right_all.at[layer, source],
            send_sem=core_send_sem.at[layer, step],
            recv_sem=core_recv_sem.at[layer, step],
            device_id={"row": other_core},
            device_id_type=MESH,
        )

    def layer_copy(n):
        if n == 0:
            source, target = triples_both.at[0], triples_both.at[1]
        elif n == 1:
            source, target = right_all.at[0, row], right_all.at[1, row]
        else:
            source, target = left_all.at[chunks - hybrid + n - 2, col], left_all.at[chunks + n - 2, col]
        return pltpu.make_async_remote_copy(
            src_ref=source,
            dst_ref=target,
            send_sem=layer_send_sem.at[n],
            recv_sem=layer_recv_sem.at[n],
            device_id={"depth": turn(depth, 1, n_depth)},
            device_id_type=MESH,
        )

    def chunk_parts(q):
        return [q] if q < chunks - hybrid else [q, q + hybrid]

    def begin(q):
        for part in chunk_parts(q):
            if part >= chunks:
                layer_copy(part - chunks + 2).wait_recv()
            left_start(part, 0)

    def part_copy(q, step, half):
        piece = pl.ds(half * (pairs // HALVES), pairs // HALVES)
        return pltpu.make_async_remote_copy(
            src_ref=part_send.at[q, step - 1, piece],
            dst_ref=part_recv.at[q, step - 1, piece],
            send_sem=part_send_sem.at[q, step - 1, half],
            recv_sem=part_recv_sem.at[q, step - 1, half],
            device_id={"depth": turn(depth, step, n_depth)},
            device_id_type=MESH,
        )

    for step in range(1, outers):
        right_copy(0, step).start()
    left_start(0, 0)
    core_copy(0, 0).start()
    fetches[2].wait()
    layers = 2 if hybrid else 1
    if hybrid:
        for n in range(hybrid + 2):
            layer_copy(n).start()
    begin(1)

    lane = lax.broadcasted_iota(jnp.int32, (16, width), 1)
    code_lane = lax.broadcasted_iota(jnp.int32, (16, LANES), 1)

    def tabulate(layer):
        left_slot = triples_both[layer, 0:1, :]
        right_slot = triples_both[layer, 1:2, :]
        out_slot = triples_both[layer, 2:3, :]
        group_of = lax.rem(left_slot, groups)
        block_row = lax.div(left_slot, groups)
        block_col = lax.div(right_slot, groups)
        for k in range(0, PC, 16):
            here = out_slot == lax.broadcasted_iota(jnp.int32, (16, out_slot.shape[1]), 0) + k
            at_row = jnp.max(jnp.where(here, block_row, 0), axis=1, keepdims=True)
            at_col = jnp.max(jnp.where(here, block_col, 0), axis=1, keepdims=True)
            code_rows[layer, k : k + 16, :] = jnp.where(code_lane == 0, at_row, at_col)
            used = jnp.zeros((16, width), jnp.float32)
            for g in range(groups):
                at_group = jnp.max(
                    jnp.where(here & (group_of == g), 1.0, 0.0).astype(jnp.float32), axis=1, keepdims=True
                )
                used = jnp.where(lane // order == g, at_group, used)
            mask_rows[layer, k : k + 16, :] = used
        code_copy = pltpu.make_async_copy(code_rows.at[layer], codes.at[layer], code_sem.at[layer])
        code_copy.start()

        def spread(k, carry):
            mask_ref[layer, k] = jnp.broadcast_to(
                mask_rows[layer, pl.ds(k, 1), :], (CHUNK_ROWS, width)
            ).astype(jnp.bfloat16)
            return carry

        lax.fori_loop(0, PC, spread, 0, unroll=8)
        code_copy.wait()

    tabulate(0)
    if hybrid:
        layer_copy(0).wait_recv()
        tabulate(1)

    lower = lax.broadcasted_iota(jnp.int32, (order, LANES), 1) < order

    def split_right(layer, shard):
        for j in range(local_rows // 2):
            for g in range(groups):
                rows = slice(g * order, (g + 1) * order)
                value = right_all[layer, shard, j, rows, :]
                high = value.astype(jnp.bfloat16).astype(jnp.float32)
                low = pltpu.roll(value - high, order, 1)
                at = shard * local_rows + 2 * j
                right_split[layer, at, rows, :] = jnp.where(lower, high, low).astype(jnp.bfloat16)
                right_split[layer, at + 1, rows, :] = jnp.where(lower, low, high).astype(jnp.bfloat16)

    for hops in range(1, n_col - 1):
        left_arrive(0, hops)
    split_right(0, row)
    core_copy(0, 0).wait_recv()
    split_right(0, other_core)

    def right_pass(layer, split):
        for step in range(1, outers):
            right_copy(layer, step).wait_recv()
            core_copy(layer, step).start()
            if split:
                split_right(layer, turn(outer + outers, -step, outers) * 2 + core)

    def right_last(layer):
        for step in range(1, outers):
            core_copy(layer, step).wait_recv()
            split_right(layer, turn(outer + outers, -step, outers) * 2 + (1 - core))

    right_pass(0, True)
    if hybrid:
        layer_copy(1).wait_recv()
        for step in range(1, outers):
            right_copy(1, step).start()
        core_copy(1, 0).start()
    right_last(0)

    lane_low = lax.broadcasted_iota(jnp.int32, (CHUNK_ROWS, LANES), 1) < order

    def one_slot(layer, q, k):
        picked = left_split[q, codes[layer, k, 0]]
        used = mask_ref[layer, k]
        picked = picked * jnp.concatenate([used, used], axis=0)
        both = jnp.dot(picked, right_split[layer, codes[layer, k, 1]], preferred_element_type=jnp.float32)
        both = both[:CHUNK_ROWS] + both[CHUNK_ROWS:]
        return both + pltpu.roll(both, order, 1)

    def products(parts, first, target, half):
        def body(turn_index, carry):
            for inner in range(UNROLL_PAIRS):
                p = turn_index * UNROLL_PAIRS + inner
                k = first + 2 * p
                total = None
                for layer, part in enumerate(parts):
                    pair = jnp.where(lane_low, one_slot(layer, part, k), one_slot(layer, part, k + 1))
                    total = pair if total is None else total + pair
                target[p] = total
            return carry

        turns = pairs // UNROLL_PAIRS // HALVES
        lax.fori_loop(half * turns, (half + 1) * turns, body, 0)

    def finish(q):
        sent = range(1, n_depth) if q < chunks - hybrid else range(0)
        for step in sent:
            for half in range(HALVES):
                part_copy(q, step, half).wait_recv()

        def body(p, carry):
            total = part_own[q, p]
            for step in sent:
                total = total + part_recv[q, step - 1, p]
            rows = pl.ds(q * CHUNK_ROWS, CHUNK_ROWS)
            out_ref[2 * p, rows, :] = total[:, :order]
            out_ref[2 * p + 1, rows, :] = pltpu.roll(total, order, 1)[:, :order]
            return carry

        lax.fori_loop(0, pairs, body, 0, unroll=min(8, pairs))

    for q in range(chunks):
        for part in chunk_parts(q):
            left_arrive(part, n_col - 1)
        if q + 2 < chunks:
            begin(q + 2)
        for part in chunk_parts(q):
            for shard in range(n_col):
                for i in range(local_rows):
                    high, low = split_bf16(left_all[part, shard, i])
                    left_split[part, shard * local_rows + i, :CHUNK_ROWS, :] = high
                    left_split[part, shard * local_rows + i, CHUNK_ROWS:, :] = low
        if q < chunks - hybrid:
            for step in range(1, n_depth):
                partner = turn(depth, step, n_depth)
                for half in range(HALVES):
                    products([q], partner * share, part_send.at[q, step - 1], half)
                    part_copy(q, step, half).start()
        hops_ahead = range(1, n_col - 1) if q + 1 < chunks else range(0)
        for half in range(HALVES):
            for hops in hops_ahead[half::HALVES]:
                for part in chunk_parts(q + 1):
                    left_arrive(part, hops)
            products(chunk_parts(q), depth * share, part_own.at[q], half)
        if hybrid and q == 0:
            right_pass(1, False)
        if hybrid and q == 1:
            core_copy(1, 0).wait_recv()
            right_last(1)
            split_right(1, row)
            split_right(1, other_core)
            for step in range(1, outers):
                split_right(1, turn(outer + outers, -step, outers) * 2 + core)
        if q > 0 and q < chunks - hybrid:
            finish(q - 1)
    for q in range(max(0, chunks - hybrid - 1), chunks):
        finish(q)

    for q in range(chunks):
        for part in chunk_parts(q):
            for hops in range(n_col - 1):
                for way in (1, -1):
                    along(way, hops, lambda shard: left_copy(part, shard, way, hops).wait_send())
        if q < chunks - hybrid:
            for step in range(1, n_depth):
                for half in range(HALVES):
                    part_copy(q, step, half).wait_send()
    for layer in range(layers):
        for step in range(1, outers):
            right_copy(layer, step).wait_send()
        for step in range(outers):
            core_copy(layer, step).wait_send()
    if hybrid:
        for n in range(hybrid + 2):
            layer_copy(n).wait_send()


def per_device(sizes, left_blocks, right_blocks, triples):
    n_row, n_col, n_depth, order, groups, local_rows, share, chunks, hybrid = sizes
    width = groups * order
    pairs = share // 2
    layers = 2 if hybrid else 1
    f32, bf16, i32 = jnp.float32, jnp.bfloat16, jnp.int32
    dma = pltpu.SemaphoreType.DMA
    return pl.pallas_call(
        functools.partial(kernel, sizes),
        out_shape=jax.ShapeDtypeStruct((share, order, order), f32),
        in_specs=[pl.BlockSpec(memory_space=pl.ANY)] * 3,
        out_specs=pl.BlockSpec(memory_space=pltpu.VMEM),
        scratch_shapes=[
            pltpu.VMEM(left_blocks.shape, f32),
            pltpu.VMEM(right_blocks.shape, f32),
            pltpu.VMEM((layers,) + triples.shape, i32),
            pltpu.VMEM((chunks + hybrid, n_col, local_rows, CHUNK_ROWS, width), f32),
            pltpu.VMEM((layers, n_row, local_rows // 2, width, LANES), f32),
            pltpu.VMEM((layers, n_row * local_rows, width, LANES), bf16),
            pltpu.VMEM((chunks + hybrid, n_col * local_rows, 2 * CHUNK_ROWS, width), bf16),
            pltpu.VMEM((layers, PC, CHUNK_ROWS, width), bf16),
            pltpu.VMEM((layers, PC, width), f32),
            pltpu.VMEM((layers, PC, LANES), i32),
            pltpu.SMEM((layers, PC, LANES), i32),
            pltpu.VMEM((chunks, n_depth - 1, pairs, CHUNK_ROWS, LANES), f32),
            pltpu.VMEM((chunks, n_depth - 1, pairs, CHUNK_ROWS, LANES), f32),
            pltpu.VMEM((chunks, pairs, CHUNK_ROWS, LANES), f32),
            dma((chunks + hybrid, 2, n_col - 1)),
            dma((chunks + hybrid, 2, n_col - 1)),
            dma((layers, n_row // 2 - 1)),
            dma((layers, n_row // 2 - 1)),
            dma((layers, n_row // 2)),
            dma((layers, n_row // 2)),
            dma((chunks, n_depth - 1, HALVES)),
            dma((chunks, n_depth - 1, HALVES)),
            dma((layers,)),
            dma((3,)),
            dma((hybrid + 2,)),
            dma((hybrid + 2,)),
        ],
        compiler_params=pltpu.CompilerParams(
            collective_id=0, has_side_effects=True, vmem_limit_bytes=48 * 1024 * 1024
        ),
        cost_estimate=pl.CostEstimate(
            flops=2 * PC * 4 * order * width * order, bytes_accessed=8 * 1024 * 1024, transcendentals=0
        ),
        name="filtered_product",
    )(*(pltpu.with_memory_space_constraint(x, pltpu.HBM) for x in (left_blocks, right_blocks, triples)))


def solution(mesh):
    n_row, n_col, n_depth = mesh.shape["row"], mesh.shape["col"], mesh.shape["depth"]
    devices = n_row * n_col * n_depth
    placed = (
        P(("row", "col", "depth"), None, None),
        P(("row", "col", "depth"), None, None),
        P(None, ("row", "col", "depth")),
    )

    def whole(left_blocks, right_blocks, triples):
        local = left_blocks.shape[0] // devices
        order = left_blocks.shape[1]
        groups = max(1, local // 4)
        chunks = order // CHUNK_ROWS
        hybrid = HYBRID if n_depth == 2 and chunks >= HYBRID + 2 else 0
        sizes = (n_row, n_col, n_depth, order, groups, local // groups, PC // n_depth, chunks, hybrid)
        return jax.shard_map(
            functools.partial(per_device, sizes),
            mesh=mesh,
            in_specs=placed,
            out_specs=P(("row", "col", "depth"), None, None),
            check_vma=False,
        )(left_blocks, right_blocks, triples)

    return whole
```

```python
import functools
import math

import jax
import jax.numpy as jnp
from jax import lax
from jax.experimental import pallas as pl
from jax.experimental.pallas import tpu as pltpu
from jax.sharding import PartitionSpec as P

PC = 128
LANES = 128
CHUNK_ROWS = 16
UNROLL_PAIRS = 16
HALVES = 2
HYBRID = 1
MESH = pl.DeviceIdType.MESH


def split_bf16(value):
    high = value.astype(jnp.bfloat16)
    low = (value - high.astype(jnp.float32)).astype(jnp.bfloat16)
    return high, low


def kernel(
    sizes,
    left_hbm,
    right_hbm,
    triples_hbm,
    out_ref,
    left_ref,
    right_ref,
    triples_both,
    left_all,
    right_all,
    right_split,
    left_split,
    mask_ref,
    mask_rows,
    code_rows,
    codes,
    part_send,
    part_recv,
    part_own,
    left_send_sem,
    left_recv_sem,
    right_send_sem,
    right_recv_sem,
    core_send_sem,
    core_recv_sem,
    part_send_sem,
    part_recv_sem,
    code_sem,
    in_sem,
    layer_send_sem,
    layer_recv_sem,
):
    n_row, n_col, n_depth, order, groups, local_rows, share, chunks, hybrid = sizes
    row = lax.axis_index("row")
    col = lax.axis_index("col")
    depth = lax.axis_index("depth")
    outers = n_row // 2
    core = row % 2
    outer = row // 2
    other_core = outer * 2 + (1 - core)
    width = groups * order
    pairs = share // 2

    def turn(index, step, count):
        return lax.rem(index + step, count)

    fetches = [
        pltpu.make_async_copy(source, target, in_sem.at[n])
        for n, (source, target) in enumerate(
            ((right_hbm, right_ref), (left_hbm, left_ref), (triples_hbm, triples_both.at[0]))
        )
    ]
    for fetch in fetches:
        fetch.start()

    barrier = pltpu.get_barrier_semaphore()
    greeted = 0
    for step in range(1, n_col):
        pl.semaphore_signal(barrier, inc=1, device_id={"col": turn(col, step, n_col)}, device_id_type=MESH)
        greeted += 1
    for step in range(1, outers):
        pl.semaphore_signal(
            barrier, inc=1, device_id={"row": turn(outer, step, outers) * 2 + core}, device_id_type=MESH
        )
        greeted += 1
    pl.semaphore_signal(barrier, inc=1, device_id={"row": other_core}, device_id_type=MESH)
    greeted += 1
    for step in range(1, n_depth):
        pl.semaphore_signal(barrier, inc=1, device_id={"depth": turn(depth, step, n_depth)}, device_id_type=MESH)
        greeted += 1

    fetches[0].wait()
    for j in range(0, local_rows, 2):
        for g in range(groups):
            pair = jnp.concatenate([right_ref[j * groups + g], right_ref[(j + 1) * groups + g]], axis=-1)
            right_all[0, row, j // 2, g * order : (g + 1) * order, :] = pair
    fetches[1].wait()
    for i in range(local_rows):
        for g in range(0, groups, 2):
            pair = jnp.concatenate([left_ref[i * groups + g], left_ref[i * groups + g + 1]], axis=-1)
            for q in range(chunks):
                left_all[q, col, i, :, g * order : (g + 2) * order] = pair[q * CHUNK_ROWS : (q + 1) * CHUNK_ROWS]

    pl.semaphore_wait(barrier, greeted)

    def left_copy(q, shard, way, hops):
        return pltpu.make_async_remote_copy(
            src_ref=left_all.at[q, shard],
            dst_ref=left_all.at[q, shard],
            send_sem=left_send_sem.at[q, max(way, 0), hops],
            recv_sem=left_recv_sem.at[q, max(way, 0), hops],
            device_id={"col": turn(col + n_col, way, n_col)},
            device_id_type=MESH,
        )

    def along(way, hops, act):
        shard = col - way * hops
        ahead = col + way
        held = jnp.logical_and(shard >= 0, shard < n_col)

        @pl.when(jnp.logical_and(held, jnp.logical_and(ahead >= 0, ahead < n_col)))
        def _():
            act(shard)

    def left_start(q, hops):
        for way in (1, -1):
            along(way, hops, lambda shard: left_copy(q, shard, way, hops).start())

    def left_arrive(q, hops):
        for way in (1, -1):
            shard = col - way * hops

            @pl.when(jnp.logical_and(shard >= 0, shard < n_col))
            def _():
                left_copy(q, shard, way, hops - 1).wait_recv()

            along(way, hops, lambda shard: left_copy(q, shard, way, hops).start())

    def right_copy(layer, step):
        return pltpu.make_async_remote_copy(
            src_ref=right_all.at[layer, row],
            dst_ref=right_all.at[layer, row],
            send_sem=right_send_sem.at[layer, step - 1],
            recv_sem=right_recv_sem.at[layer, step - 1],
            device_id={"row": turn(outer, step, outers) * 2 + core},
            device_id_type=MESH,
        )

    def core_copy(layer, step):
        source = turn(outer + outers, -step, outers) * 2 + core
        return pltpu.make_async_remote_copy(
            src_ref=right_all.at[layer, source],
            dst_ref=right_all.at[layer, source],
            send_sem=core_send_sem.at[layer, step],
            recv_sem=core_recv_sem.at[layer, step],
            device_id={"row": other_core},
            device_id_type=MESH,
        )

    def layer_copy(n):
        if n == 0:
            source, target = triples_both.at[0], triples_both.at[1]
        elif n == 1:
            source, target = right_all.at[0, row], right_all.at[1, row]
        else:
            source, target = left_all.at[chunks - hybrid + n - 2, col], left_all.at[chunks + n - 2, col]
        return pltpu.make_async_remote_copy(
            src_ref=source,
            dst_ref=target,
            send_sem=layer_send_sem.at[n],
            recv_sem=layer_recv_sem.at[n],
            device_id={"depth": turn(depth, 1, n_depth)},
            device_id_type=MESH,
        )

    def chunk_parts(q):
        return [q] if q < chunks - hybrid else [q, q + hybrid]

    def begin(q):
        for part in chunk_parts(q):
            if part >= chunks:
                layer_copy(part - chunks + 2).wait_recv()
            left_start(part, 0)

    def part_copy(q, step, half):
        piece = pl.ds(half * (pairs // HALVES), pairs // HALVES)
        return pltpu.make_async_remote_copy(
            src_ref=part_send.at[q, step - 1, piece],
            dst_ref=part_recv.at[q, step - 1, piece],
            send_sem=part_send_sem.at[q, step - 1, half],
            recv_sem=part_recv_sem.at[q, step - 1, half],
            device_id={"depth": turn(depth, step, n_depth)},
            device_id_type=MESH,
        )

    for step in range(1, outers):
        right_copy(0, step).start()
    left_start(0, 0)
    core_copy(0, 0).start()
    fetches[2].wait()
    layers = 2 if hybrid else 1
    if hybrid:
        for n in range(hybrid + 2):
            layer_copy(n).start()
    begin(1)

    lane = lax.broadcasted_iota(jnp.int32, (16, width), 1)
    code_lane = lax.broadcasted_iota(jnp.int32, (16, LANES), 1)

    def tabulate(layer):
        left_slot = triples_both[layer, 0:1, :]
        right_slot = triples_both[layer, 1:2, :]
        out_slot = triples_both[layer, 2:3, :]
        group_of = lax.rem(left_slot, groups)
        block_row = lax.div(left_slot, groups)
        block_col = lax.div(right_slot, groups)
        for k in range(0, PC, 16):
            here = out_slot == lax.broadcasted_iota(jnp.int32, (16, out_slot.shape[1]), 0) + k
            at_row = jnp.max(jnp.where(here, block_row, 0), axis=1, keepdims=True)
            at_col = jnp.max(jnp.where(here, block_col, 0), axis=1, keepdims=True)
            code_rows[layer, k : k + 16, :] = jnp.where(code_lane == 0, at_row, at_col)
            used = jnp.zeros((16, width), jnp.float32)
            for g in range(groups):
                at_group = jnp.max(
                    jnp.where(here & (group_of == g), 1.0, 0.0).astype(jnp.float32), axis=1, keepdims=True
                )
                used = jnp.where(lane // order == g, at_group, used)
            mask_rows[layer, k : k + 16, :] = used
        code_copy = pltpu.make_async_copy(code_rows.at[layer], codes.at[layer], code_sem.at[layer])
        code_copy.start()

        def spread(k, carry):
            mask_ref[layer, k] = jnp.broadcast_to(
                mask_rows[layer, pl.ds(k, 1), :], (CHUNK_ROWS, width)
            ).astype(jnp.bfloat16)
            return carry

        lax.fori_loop(0, PC, spread, 0, unroll=8)
        code_copy.wait()

    tabulate(0)
    first_hops = list(range(1, n_col - 1))
    for hops in first_hops[:1]:
        left_arrive(0, hops)
    if hybrid:
        layer_copy(0).wait_recv()
        tabulate(1)

    lower = lax.broadcasted_iota(jnp.int32, (order, LANES), 1) < order

    def split_right(layer, shard):
        for j in range(local_rows // 2):
            for g in range(groups):
                rows = slice(g * order, (g + 1) * order)
                value = right_all[layer, shard, j, rows, :]
                high = value.astype(jnp.bfloat16).astype(jnp.float32)
                low = pltpu.roll(value - high, order, 1)
                at = shard * local_rows + 2 * j
                right_split[layer, at, rows, :] = jnp.where(lower, high, low).astype(jnp.bfloat16)
                right_split[layer, at + 1, rows, :] = jnp.where(lower, low, high).astype(jnp.bfloat16)

    for hops in first_hops[1:]:
        left_arrive(0, hops)
    split_right(0, row)
    core_copy(0, 0).wait_recv()
    split_right(0, other_core)

    def right_pass(layer, split):
        for step in range(1, outers):
            right_copy(layer, step).wait_recv()
            core_copy(layer, step).start()
            if split:
                split_right(layer, turn(outer + outers, -step, outers) * 2 + core)

    def right_last(layer):
        for step in range(1, outers):
            core_copy(layer, step).wait_recv()
            split_right(layer, turn(outer + outers, -step, outers) * 2 + (1 - core))

    right_pass(0, True)
    if hybrid:
        layer_copy(1).wait_recv()
        for step in range(1, outers):
            right_copy(1, step).start()
        core_copy(1, 0).start()
    right_last(0)

    lane_low = lax.broadcasted_iota(jnp.int32, (CHUNK_ROWS, LANES), 1) < order

    def one_slot(layer, q, k):
        picked = left_split[q, codes[layer, k, 0]]
        used = mask_ref[layer, k]
        picked = picked * jnp.concatenate([used, used], axis=0)
        both = jnp.dot(picked, right_split[layer, codes[layer, k, 1]], preferred_element_type=jnp.float32)
        return both[:CHUNK_ROWS] + both[CHUNK_ROWS:]

    unroll = math.gcd(UNROLL_PAIRS, pairs // HALVES)

    def products(parts, first, target, half):
        def body(turn_index, carry):
            for inner in range(unroll):
                p = turn_index * unroll + inner
                k = first + 2 * p
                total = None
                for layer, part in enumerate(parts):
                    even, odd = one_slot(layer, part, k), one_slot(layer, part, k + 1)
                    straight = jnp.where(lane_low, even, odd)
                    crossed = jnp.where(lane_low, odd, even)
                    total = [straight, crossed] if total is None else [total[0] + straight, total[1] + crossed]
                target[p] = total[0] + pltpu.roll(total[1], order, 1)
            return carry

        turns = pairs // HALVES // unroll
        lax.fori_loop(half * turns, (half + 1) * turns, body, 0)

    def finish(q):
        sent = range(1, n_depth) if q < chunks - hybrid else range(0)
        for step in sent:
            for half in range(HALVES):
                part_copy(q, step, half).wait_recv()

        def body(p, carry):
            total = part_own[q, p]
            for step in sent:
                total = total + part_recv[q, step - 1, p]
            rows = pl.ds(q * CHUNK_ROWS, CHUNK_ROWS)
            out_ref[2 * p, rows, :] = total[:, :order]
            out_ref[2 * p + 1, rows, :] = pltpu.roll(total, order, 1)[:, :order]
            return carry

        lax.fori_loop(0, pairs, body, 0, unroll=min(8, pairs))

    for q in range(chunks):
        for part in chunk_parts(q):
            left_arrive(part, n_col - 1)
        if q + 2 < chunks:
            begin(q + 2)
        for part in chunk_parts(q):
            for shard in range(n_col):
                for i in range(local_rows):
                    high, low = split_bf16(left_all[part, shard, i])
                    left_split[part, shard * local_rows + i, :CHUNK_ROWS, :] = high
                    left_split[part, shard * local_rows + i, CHUNK_ROWS:, :] = low
        if q < chunks - hybrid:
            for step in range(1, n_depth):
                partner = turn(depth, step, n_depth)
                for half in range(HALVES):
                    products([q], partner * share, part_send.at[q, step - 1], half)
                    part_copy(q, step, half).start()
        hops_ahead = range(1, n_col - 1) if q + 1 < chunks else range(0)
        for half in range(HALVES):
            for hops in hops_ahead[half::HALVES]:
                for part in chunk_parts(q + 1):
                    left_arrive(part, hops)
            products(chunk_parts(q), depth * share, part_own.at[q], half)
        if hybrid and q == 0:
            right_pass(1, False)
        if hybrid and q == 1:
            core_copy(1, 0).wait_recv()
            right_last(1)
            split_right(1, row)
            split_right(1, other_core)
            for step in range(1, outers):
                split_right(1, turn(outer + outers, -step, outers) * 2 + core)
        if q > 0 and q < chunks - hybrid:
            finish(q - 1)
    for q in range(max(0, chunks - hybrid - 1), chunks):
        finish(q)

    for q in range(chunks):
        for part in chunk_parts(q):
            for hops in range(n_col - 1):
                for way in (1, -1):
                    along(way, hops, lambda shard: left_copy(part, shard, way, hops).wait_send())
        if q < chunks - hybrid:
            for step in range(1, n_depth):
                for half in range(HALVES):
                    part_copy(q, step, half).wait_send()
    for layer in range(layers):
        for step in range(1, outers):
            right_copy(layer, step).wait_send()
        for step in range(outers):
            core_copy(layer, step).wait_send()
    if hybrid:
        for n in range(hybrid + 2):
            layer_copy(n).wait_send()


def per_device(sizes, left_blocks, right_blocks, triples):
    n_row, n_col, n_depth, order, groups, local_rows, share, chunks, hybrid = sizes
    width = groups * order
    pairs = share // 2
    layers = 2 if hybrid else 1
    f32, bf16, i32 = jnp.float32, jnp.bfloat16, jnp.int32
    dma = pltpu.SemaphoreType.DMA
    return pl.pallas_call(
        functools.partial(kernel, sizes),
        out_shape=jax.ShapeDtypeStruct((share, order, order), f32),
        in_specs=[pl.BlockSpec(memory_space=pl.ANY)] * 3,
        out_specs=pl.BlockSpec(memory_space=pltpu.VMEM),
        scratch_shapes=[
            pltpu.VMEM(left_blocks.shape, f32),
            pltpu.VMEM(right_blocks.shape, f32),
            pltpu.VMEM((layers,) + triples.shape, i32),
            pltpu.VMEM((chunks + hybrid, n_col, local_rows, CHUNK_ROWS, width), f32),
            pltpu.VMEM((layers, n_row, local_rows // 2, width, LANES), f32),
            pltpu.VMEM((layers, n_row * local_rows, width, LANES), bf16),
            pltpu.VMEM((chunks + hybrid, n_col * local_rows, 2 * CHUNK_ROWS, width), bf16),
            pltpu.VMEM((layers, PC, CHUNK_ROWS, width), bf16),
            pltpu.VMEM((layers, PC, width), f32),
            pltpu.VMEM((layers, PC, LANES), i32),
            pltpu.SMEM((layers, PC, LANES), i32),
            pltpu.VMEM((chunks, n_depth - 1, pairs, CHUNK_ROWS, LANES), f32),
            pltpu.VMEM((chunks, n_depth - 1, pairs, CHUNK_ROWS, LANES), f32),
            pltpu.VMEM((chunks, pairs, CHUNK_ROWS, LANES), f32),
            dma((chunks + hybrid, 2, n_col - 1)),
            dma((chunks + hybrid, 2, n_col - 1)),
            dma((layers, n_row // 2 - 1)),
            dma((layers, n_row // 2 - 1)),
            dma((layers, n_row // 2)),
            dma((layers, n_row // 2)),
            dma((chunks, n_depth - 1, HALVES)),
            dma((chunks, n_depth - 1, HALVES)),
            dma((layers,)),
            dma((3,)),
            dma((hybrid + 2,)),
            dma((hybrid + 2,)),
        ],
        compiler_params=pltpu.CompilerParams(
            collective_id=0, has_side_effects=True, vmem_limit_bytes=48 * 1024 * 1024
        ),
        cost_estimate=pl.CostEstimate(
            flops=2 * PC * 4 * order * width * order, bytes_accessed=8 * 1024 * 1024, transcendentals=0
        ),
        name="filtered_product",
    )(*(pltpu.with_memory_space_constraint(x, pltpu.HBM) for x in (left_blocks, right_blocks, triples)))


def solution(mesh):
    n_row, n_col, n_depth = mesh.shape["row"], mesh.shape["col"], mesh.shape["depth"]
    devices = n_row * n_col * n_depth
    placed = (
        P(("row", "col", "depth"), None, None),
        P(("row", "col", "depth"), None, None),
        P(None, ("row", "col", "depth")),
    )

    def whole(left_blocks, right_blocks, triples):
        local = left_blocks.shape[0] // devices
        order = left_blocks.shape[1]
        groups = max(1, local // 4)
        chunks = order // CHUNK_ROWS
        hybrid = HYBRID if n_depth == 2 and chunks >= HYBRID + 2 else 0
        sizes = (n_row, n_col, n_depth, order, groups, local // groups, PC // n_depth, chunks, hybrid)
        return jax.shard_map(
            functools.partial(per_device, sizes),
            mesh=mesh,
            in_specs=placed,
            out_specs=P(("row", "col", "depth"), None, None),
            check_vma=False,
        )(left_blocks, right_blocks, triples)

    return whole
```

```python
import functools
import math

import jax
import jax.numpy as jnp
from jax import lax
from jax.experimental import pallas as pl
from jax.experimental.pallas import tpu as pltpu
from jax.sharding import PartitionSpec as P

PC = 128
LANES = 128
CHUNK_ROWS = 16
UNROLL_PAIRS = 16
HALVES = 2
HYBRID = 1
MESH = pl.DeviceIdType.MESH


def split_bf16(value):
    high = value.astype(jnp.bfloat16)
    low = (value - high.astype(jnp.float32)).astype(jnp.bfloat16)
    return high, low


def kernel(
    sizes,
    left_hbm,
    right_hbm,
    triples_hbm,
    out_ref,
    left_ref,
    right_ref,
    triples_both,
    left_all,
    right_all,
    right_split,
    left_split,
    mask_ref,
    mask_rows,
    code_rows,
    codes,
    part_send,
    part_recv,
    part_own,
    left_send_sem,
    left_recv_sem,
    right_send_sem,
    right_recv_sem,
    core_send_sem,
    core_recv_sem,
    part_send_sem,
    part_recv_sem,
    code_sem,
    in_sem,
    layer_send_sem,
    layer_recv_sem,
):
    n_row, n_col, n_depth, order, groups, local_rows, share, chunks, hybrid = sizes
    row = lax.axis_index("row")
    col = lax.axis_index("col")
    depth = lax.axis_index("depth")
    outers = n_row // 2
    core = row % 2
    outer = row // 2
    other_core = outer * 2 + (1 - core)
    width = groups * order
    pairs = share // 2

    def turn(index, step, count):
        return lax.rem(index + step, count)

    fetches = [
        pltpu.make_async_copy(source, target, in_sem.at[n])
        for n, (source, target) in enumerate(
            ((right_hbm, right_ref), (left_hbm, left_ref), (triples_hbm, triples_both.at[0]))
        )
    ]
    for fetch in fetches:
        fetch.start()

    barrier = pltpu.get_barrier_semaphore()
    greeted = 0
    for step in range(1, n_col):
        pl.semaphore_signal(barrier, inc=1, device_id={"col": turn(col, step, n_col)}, device_id_type=MESH)
        greeted += 1
    for step in range(1, outers):
        pl.semaphore_signal(
            barrier, inc=1, device_id={"row": turn(outer, step, outers) * 2 + core}, device_id_type=MESH
        )
        greeted += 1
    pl.semaphore_signal(barrier, inc=1, device_id={"row": other_core}, device_id_type=MESH)
    greeted += 1
    for step in range(1, n_depth):
        pl.semaphore_signal(barrier, inc=1, device_id={"depth": turn(depth, step, n_depth)}, device_id_type=MESH)
        greeted += 1

    fetches[0].wait()
    for j in range(0, local_rows, 2):
        for g in range(groups):
            pair = jnp.concatenate([right_ref[j * groups + g], right_ref[(j + 1) * groups + g]], axis=-1)
            right_all[0, row, j // 2, g * order : (g + 1) * order, :] = pair
    pl.semaphore_wait(barrier, greeted)

    def left_copy(q, shard, way, hops):
        return pltpu.make_async_remote_copy(
            src_ref=left_all.at[q, shard],
            dst_ref=left_all.at[q, shard],
            send_sem=left_send_sem.at[q, max(way, 0), hops],
            recv_sem=left_recv_sem.at[q, max(way, 0), hops],
            device_id={"col": turn(col + n_col, way, n_col)},
            device_id_type=MESH,
        )

    def along(way, hops, act):
        shard = col - way * hops
        ahead = col + way
        held = jnp.logical_and(shard >= 0, shard < n_col)

        @pl.when(jnp.logical_and(held, jnp.logical_and(ahead >= 0, ahead < n_col)))
        def _():
            act(shard)

    def left_start(q, hops):
        for way in (1, -1):
            along(way, hops, lambda shard: left_copy(q, shard, way, hops).start())

    def left_arrive(q, hops):
        for way in (1, -1):
            shard = col - way * hops

            @pl.when(jnp.logical_and(shard >= 0, shard < n_col))
            def _():
                left_copy(q, shard, way, hops - 1).wait_recv()

            along(way, hops, lambda shard: left_copy(q, shard, way, hops).start())

    def right_copy(layer, step):
        return pltpu.make_async_remote_copy(
            src_ref=right_all.at[layer, row],
            dst_ref=right_all.at[layer, row],
            send_sem=right_send_sem.at[layer, step - 1],
            recv_sem=right_recv_sem.at[layer, step - 1],
            device_id={"row": turn(outer, step, outers) * 2 + core},
            device_id_type=MESH,
        )

    def core_copy(layer, step):
        source = turn(outer + outers, -step, outers) * 2 + core
        return pltpu.make_async_remote_copy(
            src_ref=right_all.at[layer, source],
            dst_ref=right_all.at[layer, source],
            send_sem=core_send_sem.at[layer, step],
            recv_sem=core_recv_sem.at[layer, step],
            device_id={"row": other_core},
            device_id_type=MESH,
        )

    def layer_copy(n):
        if n == 0:
            source, target = triples_both.at[0], triples_both.at[1]
        elif n == 1:
            source, target = right_all.at[0, row], right_all.at[1, row]
        else:
            source, target = left_all.at[chunks - hybrid + n - 2, col], left_all.at[chunks + n - 2, col]
        return pltpu.make_async_remote_copy(
            src_ref=source,
            dst_ref=target,
            send_sem=layer_send_sem.at[n],
            recv_sem=layer_recv_sem.at[n],
            device_id={"depth": turn(depth, 1, n_depth)},
            device_id_type=MESH,
        )

    def chunk_parts(q):
        return [q] if q < chunks - hybrid else [q, q + hybrid]

    def begin(q):
        for part in chunk_parts(q):
            if part >= chunks:
                layer_copy(part - chunks + 2).wait_recv()
            left_start(part, 0)

    def part_copy(q, step, half):
        piece = pl.ds(half * (pairs // HALVES), pairs // HALVES)
        return pltpu.make_async_remote_copy(
            src_ref=part_send.at[q, step - 1, piece],
            dst_ref=part_recv.at[q, step - 1, piece],
            send_sem=part_send_sem.at[q, step - 1, half],
            recv_sem=part_recv_sem.at[q, step - 1, half],
            device_id={"depth": turn(depth, step, n_depth)},
            device_id_type=MESH,
        )

    for step in range(1, outers):
        right_copy(0, step).start()
    core_copy(0, 0).start()
    layers = 2 if hybrid else 1
    fetches[1].wait()
    for i in range(local_rows):
        for g in range(0, groups, 2):
            pair = jnp.concatenate([left_ref[i * groups + g], left_ref[i * groups + g + 1]], axis=-1)
            for q in range(chunks):
                left_all[q, col, i, :, g * order : (g + 2) * order] = pair[q * CHUNK_ROWS : (q + 1) * CHUNK_ROWS]
    left_start(0, 0)
    fetches[2].wait()
    if hybrid:
        for n in range(hybrid + 2):
            layer_copy(n).start()
    begin(1)

    lane = lax.broadcasted_iota(jnp.int32, (16, width), 1)
    code_lane = lax.broadcasted_iota(jnp.int32, (16, LANES), 1)

    def tabulate(layer):
        left_slot = triples_both[layer, 0:1, :]
        right_slot = triples_both[layer, 1:2, :]
        out_slot = triples_both[layer, 2:3, :]
        group_of = lax.rem(left_slot, groups)
        block_row = lax.div(left_slot, groups)
        block_col = lax.div(right_slot, groups)
        for k in range(0, PC, 16):
            here = out_slot == lax.broadcasted_iota(jnp.int32, (16, out_slot.shape[1]), 0) + k
            at_row = jnp.max(jnp.where(here, block_row, 0), axis=1, keepdims=True)
            at_col = jnp.max(jnp.where(here, block_col, 0), axis=1, keepdims=True)
            code_rows[layer, k : k + 16, :] = jnp.where(code_lane == 0, at_row, at_col)
            used = jnp.zeros((16, width), jnp.float32)
            for g in range(groups):
                at_group = jnp.max(
                    jnp.where(here & (group_of == g), 1.0, 0.0).astype(jnp.float32), axis=1, keepdims=True
                )
                used = jnp.where(lane // order == g, at_group, used)
            mask_rows[layer, k : k + 16, :] = used
        code_copy = pltpu.make_async_copy(code_rows.at[layer], codes.at[layer], code_sem.at[layer])
        code_copy.start()

        def spread(k, carry):
            mask_ref[layer, k] = jnp.broadcast_to(
                mask_rows[layer, pl.ds(k, 1), :], (CHUNK_ROWS, width)
            ).astype(jnp.bfloat16)
            return carry

        lax.fori_loop(0, PC, spread, 0, unroll=8)
        code_copy.wait()

    tabulate(0)
    first_hops = list(range(1, n_col - 1))
    for hops in first_hops[:1]:
        left_arrive(0, hops)
    if hybrid:
        layer_copy(0).wait_recv()
        tabulate(1)

    lower = lax.broadcasted_iota(jnp.int32, (order, LANES), 1) < order

    def split_right(layer, shard):
        for j in range(local_rows // 2):
            for g in range(groups):
                rows = slice(g * order, (g + 1) * order)
                value = right_all[layer, shard, j, rows, :]
                high = value.astype(jnp.bfloat16).astype(jnp.float32)
                low = pltpu.roll(value - high, order, 1)
                at = shard * local_rows + 2 * j
                right_split[layer, at, rows, :] = jnp.where(lower, high, low).astype(jnp.bfloat16)
                right_split[layer, at + 1, rows, :] = jnp.where(lower, low, high).astype(jnp.bfloat16)

    for hops in first_hops[1:]:
        left_arrive(0, hops)
    split_right(0, row)
    core_copy(0, 0).wait_recv()
    split_right(0, other_core)

    def right_pass(layer, split):
        for step in range(1, outers):
            right_copy(layer, step).wait_recv()
            core_copy(layer, step).start()
            if split:
                split_right(layer, turn(outer + outers, -step, outers) * 2 + core)

    def right_last(layer):
        for step in range(1, outers):
            core_copy(layer, step).wait_recv()
            split_right(layer, turn(outer + outers, -step, outers) * 2 + (1 - core))

    right_pass(0, True)
    if hybrid:
        layer_copy(1).wait_recv()
        for step in range(1, outers):
            right_copy(1, step).start()
        core_copy(1, 0).start()
    right_last(0)

    lane_low = lax.broadcasted_iota(jnp.int32, (CHUNK_ROWS, LANES), 1) < order

    def one_slot(layer, q, k):
        picked = left_split[q, codes[layer, k, 0]]
        used = mask_ref[layer, k]
        picked = picked * jnp.concatenate([used, used], axis=0)
        both = jnp.dot(picked, right_split[layer, codes[layer, k, 1]], preferred_element_type=jnp.float32)
        return both[:CHUNK_ROWS] + both[CHUNK_ROWS:]

    unroll = math.gcd(UNROLL_PAIRS, pairs // HALVES)

    def products(parts, first, target, half):
        def body(turn_index, carry):
            for inner in range(unroll):
                p = turn_index * unroll + inner
                k = first + 2 * p
                total = None
                for layer, part in enumerate(parts):
                    even, odd = one_slot(layer, part, k), one_slot(layer, part, k + 1)
                    straight = jnp.where(lane_low, even, odd)
                    crossed = jnp.where(lane_low, odd, even)
                    total = [straight, crossed] if total is None else [total[0] + straight, total[1] + crossed]
                target[p] = total[0] + pltpu.roll(total[1], order, 1)
            return carry

        turns = pairs // HALVES // unroll
        lax.fori_loop(half * turns, (half + 1) * turns, body, 0)

    def finish(q):
        sent = range(1, n_depth) if q < chunks - hybrid else range(0)
        for step in sent:
            for half in range(HALVES):
                part_copy(q, step, half).wait_recv()

        def body(p, carry):
            total = part_own[q, p]
            for step in sent:
                total = total + part_recv[q, step - 1, p]
            rows = pl.ds(q * CHUNK_ROWS, CHUNK_ROWS)
            out_ref[2 * p, rows, :] = total[:, :order]
            out_ref[2 * p + 1, rows, :] = pltpu.roll(total, order, 1)[:, :order]
            return carry

        lax.fori_loop(0, pairs, body, 0, unroll=min(8, pairs))

    for q in range(chunks):
        for part in chunk_parts(q):
            left_arrive(part, n_col - 1)
        if q + 2 < chunks:
            begin(q + 2)
        for part in chunk_parts(q):
            for shard in range(n_col):
                for i in range(local_rows):
                    high, low = split_bf16(left_all[part, shard, i])
                    left_split[part, shard * local_rows + i, :CHUNK_ROWS, :] = high
                    left_split[part, shard * local_rows + i, CHUNK_ROWS:, :] = low
        hops_ahead = range(1, n_col - 1) if q + 1 < chunks else range(0)
        for hops in hops_ahead[:1]:
            for part in chunk_parts(q + 1):
                left_arrive(part, hops)
        if q < chunks - hybrid:
            for step in range(1, n_depth):
                partner = turn(depth, step, n_depth)
                for half in range(HALVES):
                    products([q], partner * share, part_send.at[q, step - 1], half)
                    part_copy(q, step, half).start()
        for half in range(HALVES):
            for hops in hops_ahead[1 + half :: HALVES]:
                for part in chunk_parts(q + 1):
                    left_arrive(part, hops)
            products(chunk_parts(q), depth * share, part_own.at[q], half)
        if hybrid and q == 0:
            right_pass(1, False)
        if hybrid and q == 1:
            core_copy(1, 0).wait_recv()
            right_last(1)
            split_right(1, row)
            split_right(1, other_core)
            for step in range(1, outers):
                split_right(1, turn(outer + outers, -step, outers) * 2 + core)
        if q > 1:
            finish(q - 2)
    for q in range(max(0, chunks - 2), chunks):
        finish(q)

    for q in range(chunks):
        for part in chunk_parts(q):
            for hops in range(n_col - 1):
                for way in (1, -1):
                    along(way, hops, lambda shard: left_copy(part, shard, way, hops).wait_send())
        if q < chunks - hybrid:
            for step in range(1, n_depth):
                for half in range(HALVES):
                    part_copy(q, step, half).wait_send()
    for layer in range(layers):
        for step in range(1, outers):
            right_copy(layer, step).wait_send()
        for step in range(outers):
            core_copy(layer, step).wait_send()
    if hybrid:
        for n in range(hybrid + 2):
            layer_copy(n).wait_send()


def per_device(sizes, left_blocks, right_blocks, triples):
    n_row, n_col, n_depth, order, groups, local_rows, share, chunks, hybrid = sizes
    width = groups * order
    pairs = share // 2
    layers = 2 if hybrid else 1
    f32, bf16, i32 = jnp.float32, jnp.bfloat16, jnp.int32
    dma = pltpu.SemaphoreType.DMA
    return pl.pallas_call(
        functools.partial(kernel, sizes),
        out_shape=jax.ShapeDtypeStruct((share, order, order), f32),
        in_specs=[pl.BlockSpec(memory_space=pl.ANY)] * 3,
        out_specs=pl.BlockSpec(memory_space=pltpu.VMEM),
        scratch_shapes=[
            pltpu.VMEM(left_blocks.shape, f32),
            pltpu.VMEM(right_blocks.shape, f32),
            pltpu.VMEM((layers,) + triples.shape, i32),
            pltpu.VMEM((chunks + hybrid, n_col, local_rows, CHUNK_ROWS, width), f32),
            pltpu.VMEM((layers, n_row, local_rows // 2, width, LANES), f32),
            pltpu.VMEM((layers, n_row * local_rows, width, LANES), bf16),
            pltpu.VMEM((chunks + hybrid, n_col * local_rows, 2 * CHUNK_ROWS, width), bf16),
            pltpu.VMEM((layers, PC, CHUNK_ROWS, width), bf16),
            pltpu.VMEM((layers, PC, width), f32),
            pltpu.VMEM((layers, PC, LANES), i32),
            pltpu.SMEM((layers, PC, LANES), i32),
            pltpu.VMEM((chunks, n_depth - 1, pairs, CHUNK_ROWS, LANES), f32),
            pltpu.VMEM((chunks, n_depth - 1, pairs, CHUNK_ROWS, LANES), f32),
            pltpu.VMEM((chunks, pairs, CHUNK_ROWS, LANES), f32),
            dma((chunks + hybrid, 2, n_col - 1)),
            dma((chunks + hybrid, 2, n_col - 1)),
            dma((layers, n_row // 2 - 1)),
            dma((layers, n_row // 2 - 1)),
            dma((layers, n_row // 2)),
            dma((layers, n_row // 2)),
            dma((chunks, n_depth - 1, HALVES)),
            dma((chunks, n_depth - 1, HALVES)),
            dma((layers,)),
            dma((3,)),
            dma((hybrid + 2,)),
            dma((hybrid + 2,)),
        ],
        compiler_params=pltpu.CompilerParams(
            collective_id=0, has_side_effects=True, vmem_limit_bytes=48 * 1024 * 1024
        ),
        cost_estimate=pl.CostEstimate(
            flops=2 * PC * 4 * order * width * order, bytes_accessed=8 * 1024 * 1024, transcendentals=0
        ),
        name="filtered_product",
    )(*(pltpu.with_memory_space_constraint(x, pltpu.HBM) for x in (left_blocks, right_blocks, triples)))


def solution(mesh):
    n_row, n_col, n_depth = mesh.shape["row"], mesh.shape["col"], mesh.shape["depth"]
    devices = n_row * n_col * n_depth
    placed = (
        P(("row", "col", "depth"), None, None),
        P(("row", "col", "depth"), None, None),
        P(None, ("row", "col", "depth")),
    )

    def whole(left_blocks, right_blocks, triples):
        local = left_blocks.shape[0] // devices
        order = left_blocks.shape[1]
        groups = max(1, local // 4)
        chunks = order // CHUNK_ROWS
        hybrid = HYBRID if n_depth == 2 and chunks >= HYBRID + 2 else 0
        sizes = (n_row, n_col, n_depth, order, groups, local // groups, PC // n_depth, chunks, hybrid)
        return jax.shard_map(
            functools.partial(per_device, sizes),
            mesh=mesh,
            in_specs=placed,
            out_specs=P(("row", "col", "depth"), None, None),
            check_vma=False,
        )(left_blocks, right_blocks, triples)

    return whole
```

```python
import functools
import math

import jax
import jax.numpy as jnp
from jax import lax
from jax.experimental import pallas as pl
from jax.experimental.pallas import tpu as pltpu
from jax.sharding import PartitionSpec as P

PC = 128
LANES = 128
CHUNK_ROWS = 16
UNROLL_PAIRS = 16
HALVES = 2
HYBRID = 1
MESH = pl.DeviceIdType.MESH


def split_bf16(value):
    high = value.astype(jnp.bfloat16)
    low = (value - high.astype(jnp.float32)).astype(jnp.bfloat16)
    return high, low


def kernel(
    sizes,
    left_hbm,
    right_hbm,
    triples_hbm,
    out_ref,
    left_ref,
    right_ref,
    triples_both,
    left_all,
    right_all,
    right_split,
    left_split,
    mask_ref,
    mask_rows,
    code_rows,
    codes,
    part_send,
    part_recv,
    part_own,
    left_send_sem,
    left_recv_sem,
    right_send_sem,
    right_recv_sem,
    core_send_sem,
    core_recv_sem,
    part_send_sem,
    part_recv_sem,
    code_sem,
    in_sem,
    layer_send_sem,
    layer_recv_sem,
):
    n_row, n_col, n_depth, order, groups, local_rows, share, chunks, hybrid = sizes
    row = lax.axis_index("row")
    col = lax.axis_index("col")
    depth = lax.axis_index("depth")
    outers = n_row // 2
    core = row % 2
    outer = row // 2
    other_core = outer * 2 + (1 - core)
    width = groups * order
    pairs = share // 2

    def turn(index, step, count):
        return lax.rem(index + step, count)

    fetches = [
        pltpu.make_async_copy(source, target, in_sem.at[n])
        for n, (source, target) in enumerate(
            ((right_hbm, right_ref), (left_hbm, left_ref), (triples_hbm, triples_both.at[0]))
        )
    ]
    for fetch in fetches:
        fetch.start()

    barrier = pltpu.get_barrier_semaphore()
    greeted = 0
    for step in range(1, n_col):
        pl.semaphore_signal(barrier, inc=1, device_id={"col": turn(col, step, n_col)}, device_id_type=MESH)
        greeted += 1
    for step in range(1, outers):
        pl.semaphore_signal(
            barrier, inc=1, device_id={"row": turn(outer, step, outers) * 2 + core}, device_id_type=MESH
        )
        greeted += 1
    pl.semaphore_signal(barrier, inc=1, device_id={"row": other_core}, device_id_type=MESH)
    greeted += 1
    for step in range(1, n_depth):
        pl.semaphore_signal(barrier, inc=1, device_id={"depth": turn(depth, step, n_depth)}, device_id_type=MESH)
        greeted += 1

    fetches[0].wait()
    for j in range(0, local_rows, 2):
        for g in range(groups):
            pair = jnp.concatenate([right_ref[j * groups + g], right_ref[(j + 1) * groups + g]], axis=-1)
            right_all[0, row, j // 2, g * order : (g + 1) * order, :] = pair
    pl.semaphore_wait(barrier, greeted)

    def left_copy(q, shard, way, hops):
        return pltpu.make_async_remote_copy(
            src_ref=left_all.at[q, shard],
            dst_ref=left_all.at[q, shard],
            send_sem=left_send_sem.at[q, max(way, 0), hops],
            recv_sem=left_recv_sem.at[q, max(way, 0), hops],
            device_id={"col": turn(col + n_col, way, n_col)},
            device_id_type=MESH,
        )

    def along(way, hops, act):
        shard = col - way * hops
        ahead = col + way
        held = jnp.logical_and(shard >= 0, shard < n_col)

        @pl.when(jnp.logical_and(held, jnp.logical_and(ahead >= 0, ahead < n_col)))
        def _():
            act(shard)

    def left_start(q, hops):
        for way in (1, -1):
            along(way, hops, lambda shard: left_copy(q, shard, way, hops).start())

    def left_arrive(q, hops):
        for way in (1, -1):
            shard = col - way * hops

            @pl.when(jnp.logical_and(shard >= 0, shard < n_col))
            def _():
                left_copy(q, shard, way, hops - 1).wait_recv()

            along(way, hops, lambda shard: left_copy(q, shard, way, hops).start())

    def right_copy(layer, step):
        return pltpu.make_async_remote_copy(
            src_ref=right_all.at[layer, row],
            dst_ref=right_all.at[layer, row],
            send_sem=right_send_sem.at[layer, step - 1],
            recv_sem=right_recv_sem.at[layer, step - 1],
            device_id={"row": turn(outer, step, outers) * 2 + core},
            device_id_type=MESH,
        )

    def core_copy(layer, step):
        source = turn(outer + outers, -step, outers) * 2 + core
        return pltpu.make_async_remote_copy(
            src_ref=right_all.at[layer, source],
            dst_ref=right_all.at[layer, source],
            send_sem=core_send_sem.at[layer, step],
            recv_sem=core_recv_sem.at[layer, step],
            device_id={"row": other_core},
            device_id_type=MESH,
        )

    def layer_copy(n):
        if n == 0:
            source, target = triples_both.at[0], triples_both.at[1]
        elif n == 1:
            source, target = right_all.at[0, row], right_all.at[1, row]
        else:
            source, target = left_all.at[chunks - hybrid + n - 2, col], left_all.at[chunks + n - 2, col]
        return pltpu.make_async_remote_copy(
            src_ref=source,
            dst_ref=target,
            send_sem=layer_send_sem.at[n],
            recv_sem=layer_recv_sem.at[n],
            device_id={"depth": turn(depth, 1, n_depth)},
            device_id_type=MESH,
        )

    def chunk_parts(q):
        return [q] if q < chunks - hybrid else [q, q + hybrid]

    def begin(q):
        for part in chunk_parts(q):
            if part >= chunks:
                layer_copy(part - chunks + 2).wait_recv()
            left_start(part, 0)

    def part_copy(q, step, half):
        piece = pl.ds(half * (pairs // HALVES), pairs // HALVES)
        return pltpu.make_async_remote_copy(
            src_ref=part_send.at[q, step - 1, piece],
            dst_ref=part_recv.at[q, step - 1, piece],
            send_sem=part_send_sem.at[q, step - 1, half],
            recv_sem=part_recv_sem.at[q, step - 1, half],
            device_id={"depth": turn(depth, step, n_depth)},
            device_id_type=MESH,
        )

    for step in range(1, outers):
        right_copy(0, step).start()
    core_copy(0, 0).start()
    layers = 2 if hybrid else 1
    fetches[1].wait()
    for i in range(local_rows):
        for g in range(0, groups, 2):
            pair = jnp.concatenate([left_ref[i * groups + g], left_ref[i * groups + g + 1]], axis=-1)
            for q in range(chunks):
                left_all[q, col, i, :, g * order : (g + 2) * order] = pair[q * CHUNK_ROWS : (q + 1) * CHUNK_ROWS]
    left_start(0, 0)
    fetches[2].wait()
    if hybrid:
        for n in range(hybrid + 2):
            layer_copy(n).start()
    begin(1)

    lane = lax.broadcasted_iota(jnp.int32, (16, width), 1)
    code_lane = lax.broadcasted_iota(jnp.int32, (16, LANES), 1)

    def tabulate(layer):
        left_slot = triples_both[layer, 0:1, :]
        right_slot = triples_both[layer, 1:2, :]
        out_slot = triples_both[layer, 2:3, :]
        group_of = lax.rem(left_slot, groups)
        block_row = lax.div(left_slot, groups)
        block_col = lax.div(right_slot, groups)
        for k in range(0, PC, 16):
            here = out_slot == lax.broadcasted_iota(jnp.int32, (16, out_slot.shape[1]), 0) + k
            at_row = jnp.max(jnp.where(here, block_row, 0), axis=1, keepdims=True)
            at_col = jnp.max(jnp.where(here, block_col, 0), axis=1, keepdims=True)
            code_rows[layer, k : k + 16, :] = jnp.where(code_lane == 0, at_row, at_col)
            used = jnp.zeros((16, width), jnp.float32)
            for g in range(groups):
                at_group = jnp.max(
                    jnp.where(here & (group_of == g), 1.0, 0.0).astype(jnp.float32), axis=1, keepdims=True
                )
                used = jnp.where(lane // order == g, at_group, used)
            mask_rows[layer, k : k + 16, :] = used
        code_copy = pltpu.make_async_copy(code_rows.at[layer], codes.at[layer], code_sem.at[layer])
        code_copy.start()

        def spread(k, carry):
            mask_ref[layer, k] = jnp.broadcast_to(
                mask_rows[layer, pl.ds(k, 1), :], (CHUNK_ROWS, width)
            ).astype(jnp.bfloat16)
            return carry

        lax.fori_loop(0, PC, spread, 0, unroll=8)
        code_copy.wait()

    tabulate(0)
    first_hops = list(range(1, n_col - 1))
    for hops in first_hops[:1]:
        left_arrive(0, hops)
    if hybrid:
        layer_copy(0).wait_recv()
        tabulate(1)

    lower = lax.broadcasted_iota(jnp.int32, (order, LANES), 1) < order

    def split_right(layer, shard):
        for j in range(local_rows // 2):
            for g in range(groups):
                rows = slice(g * order, (g + 1) * order)
                value = right_all[layer, shard, j, rows, :]
                high = value.astype(jnp.bfloat16).astype(jnp.float32)
                low = pltpu.roll(value - high, order, 1)
                at = shard * local_rows + 2 * j
                right_split[layer, at, rows, :] = jnp.where(lower, high, low).astype(jnp.bfloat16)
                right_split[layer, at + 1, rows, :] = jnp.where(lower, low, high).astype(jnp.bfloat16)

    for hops in first_hops[1:]:
        left_arrive(0, hops)
    split_right(0, row)
    core_copy(0, 0).wait_recv()
    split_right(0, other_core)

    def right_pass(layer, split):
        for step in range(1, outers):
            right_copy(layer, step).wait_recv()
            core_copy(layer, step).start()
            if split:
                split_right(layer, turn(outer + outers, -step, outers) * 2 + core)

    def right_last(layer):
        for step in range(1, outers):
            core_copy(layer, step).wait_recv()
            split_right(layer, turn(outer + outers, -step, outers) * 2 + (1 - core))

    right_pass(0, True)
    if hybrid:
        layer_copy(1).wait_recv()
        for step in range(1, outers):
            right_copy(1, step).start()
        core_copy(1, 0).start()
    right_last(0)

    lane_low = lax.broadcasted_iota(jnp.int32, (CHUNK_ROWS, LANES), 1) < order

    def one_slot(layer, q, k):
        picked = left_split[q, codes[layer, k, 0]]
        used = mask_ref[layer, k]
        picked = picked * jnp.concatenate([used, used], axis=0)
        both = jnp.dot(picked, right_split[layer, codes[layer, k, 1]], preferred_element_type=jnp.float32)
        return both[:CHUNK_ROWS] + both[CHUNK_ROWS:]

    unroll = math.gcd(UNROLL_PAIRS, pairs // HALVES)

    def products(parts, first, target, half, unroll=unroll):
        def body(turn_index, carry):
            for inner in range(unroll):
                p = turn_index * unroll + inner
                k = first + 2 * p
                total = None
                for layer, part in enumerate(parts):
                    even, odd = one_slot(layer, part, k), one_slot(layer, part, k + 1)
                    straight = jnp.where(lane_low, even, odd)
                    crossed = jnp.where(lane_low, odd, even)
                    total = [straight, crossed] if total is None else [total[0] + straight, total[1] + crossed]
                target[p] = total[0] + pltpu.roll(total[1], order, 1)
            return carry

        turns = max(1, pairs // HALVES // unroll)
        lax.fori_loop(half * turns, (half + 1) * turns, body, 0)

    def finish(q):
        sent = range(1, n_depth) if q < chunks - hybrid else range(0)
        for step in sent:
            for half in range(HALVES):
                part_copy(q, step, half).wait_recv()

        def body(p, carry):
            total = part_own[q, p]
            for step in sent:
                total = total + part_recv[q, step - 1, p]
            rows = pl.ds(q * CHUNK_ROWS, CHUNK_ROWS)
            out_ref[2 * p, rows, :] = total[:, :order]
            out_ref[2 * p + 1, rows, :] = pltpu.roll(total, order, 1)[:, :order]
            return carry

        lax.fori_loop(0, pairs, body, 0, unroll=min(8, pairs))

    for q in range(chunks):
        for part in chunk_parts(q):
            left_arrive(part, n_col - 1)
        if q + 2 < chunks:
            begin(q + 2)
        for part in chunk_parts(q):
            for shard in range(n_col):
                for i in range(local_rows):
                    high, low = split_bf16(left_all[part, shard, i])
                    left_split[part, shard * local_rows + i, :CHUNK_ROWS, :] = high
                    left_split[part, shard * local_rows + i, CHUNK_ROWS:, :] = low
        if q < chunks - hybrid:
            for step in range(1, n_depth):
                partner = turn(depth, step, n_depth)
                for half in range(HALVES):
                    products([q], partner * share, part_send.at[q, step - 1], half)
                    part_copy(q, step, half).start()
        hops_ahead = range(1, n_col - 1) if q + 1 < chunks else range(0)
        for hops in hops_ahead:
            for part in chunk_parts(q + 1):
                left_arrive(part, hops)
        if q < chunks - hybrid:
            products([q], depth * share, part_own.at[q], 0, pairs)
        else:
            for half in range(HALVES):
                products(chunk_parts(q), depth * share, part_own.at[q], half)
        if hybrid and q == 0:
            right_pass(1, False)
        if hybrid and q == 1:
            core_copy(1, 0).wait_recv()
            right_last(1)
            split_right(1, row)
            split_right(1, other_core)
            for step in range(1, outers):
                split_right(1, turn(outer + outers, -step, outers) * 2 + core)
        if q > 0 and q < chunks - hybrid:
            finish(q - 1)
    for q in range(max(0, chunks - hybrid - 1), chunks):
        finish(q)

    for q in range(chunks):
        for part in chunk_parts(q):
            for hops in range(n_col - 1):
                for way in (1, -1):
                    along(way, hops, lambda shard: left_copy(part, shard, way, hops).wait_send())
        if q < chunks - hybrid:
            for step in range(1, n_depth):
                for half in range(HALVES):
                    part_copy(q, step, half).wait_send()
    for layer in range(layers):
        for step in range(1, outers):
            right_copy(layer, step).wait_send()
        for step in range(outers):
            core_copy(layer, step).wait_send()
    if hybrid:
        for n in range(hybrid + 2):
            layer_copy(n).wait_send()


def per_device(sizes, left_blocks, right_blocks, triples):
    n_row, n_col, n_depth, order, groups, local_rows, share, chunks, hybrid = sizes
    width = groups * order
    pairs = share // 2
    layers = 2 if hybrid else 1
    f32, bf16, i32 = jnp.float32, jnp.bfloat16, jnp.int32
    dma = pltpu.SemaphoreType.DMA
    return pl.pallas_call(
        functools.partial(kernel, sizes),
        out_shape=jax.ShapeDtypeStruct((share, order, order), f32),
        in_specs=[pl.BlockSpec(memory_space=pl.ANY)] * 3,
        out_specs=pl.BlockSpec(memory_space=pltpu.VMEM),
        scratch_shapes=[
            pltpu.VMEM(left_blocks.shape, f32),
            pltpu.VMEM(right_blocks.shape, f32),
            pltpu.VMEM((layers,) + triples.shape, i32),
            pltpu.VMEM((chunks + hybrid, n_col, local_rows, CHUNK_ROWS, width), f32),
            pltpu.VMEM((layers, n_row, local_rows // 2, width, LANES), f32),
            pltpu.VMEM((layers, n_row * local_rows, width, LANES), bf16),
            pltpu.VMEM((chunks + hybrid, n_col * local_rows, 2 * CHUNK_ROWS, width), bf16),
            pltpu.VMEM((layers, PC, CHUNK_ROWS, width), bf16),
            pltpu.VMEM((layers, PC, width), f32),
            pltpu.VMEM((layers, PC, LANES), i32),
            pltpu.SMEM((layers, PC, LANES), i32),
            pltpu.VMEM((chunks, n_depth - 1, pairs, CHUNK_ROWS, LANES), f32),
            pltpu.VMEM((chunks, n_depth - 1, pairs, CHUNK_ROWS, LANES), f32),
            pltpu.VMEM((chunks, pairs, CHUNK_ROWS, LANES), f32),
            dma((chunks + hybrid, 2, n_col - 1)),
            dma((chunks + hybrid, 2, n_col - 1)),
            dma((layers, n_row // 2 - 1)),
            dma((layers, n_row // 2 - 1)),
            dma((layers, n_row // 2)),
            dma((layers, n_row // 2)),
            dma((chunks, n_depth - 1, HALVES)),
            dma((chunks, n_depth - 1, HALVES)),
            dma((layers,)),
            dma((3,)),
            dma((hybrid + 2,)),
            dma((hybrid + 2,)),
        ],
        compiler_params=pltpu.CompilerParams(
            collective_id=0, has_side_effects=True, vmem_limit_bytes=48 * 1024 * 1024
        ),
        cost_estimate=pl.CostEstimate(
            flops=2 * PC * 4 * order * width * order, bytes_accessed=8 * 1024 * 1024, transcendentals=0
        ),
        name="filtered_product",
    )(*(pltpu.with_memory_space_constraint(x, pltpu.HBM) for x in (left_blocks, right_blocks, triples)))


def solution(mesh):
    n_row, n_col, n_depth = mesh.shape["row"], mesh.shape["col"], mesh.shape["depth"]
    devices = n_row * n_col * n_depth
    placed = (
        P(("row", "col", "depth"), None, None),
        P(("row", "col", "depth"), None, None),
        P(None, ("row", "col", "depth")),
    )

    def whole(left_blocks, right_blocks, triples):
        local = left_blocks.shape[0] // devices
        order = left_blocks.shape[1]
        groups = max(1, local // 4)
        chunks = order // CHUNK_ROWS
        hybrid = HYBRID if n_depth == 2 and chunks >= HYBRID + 2 else 0
        sizes = (n_row, n_col, n_depth, order, groups, local // groups, PC // n_depth, chunks, hybrid)
        return jax.shard_map(
            functools.partial(per_device, sizes),
            mesh=mesh,
            in_specs=placed,
            out_specs=P(("row", "col", "depth"), None, None),
            check_vma=False,
        )(left_blocks, right_blocks, triples)

    return whole
```
